128 devices in a mesh: dp: 32 (over y, x, core), mp: 4 (over z).
Axes of the slice: x: 4, y: 4, z: 4, core: 2. Of those that a mesh axis runs over, the one named last changes fastest.
Arguments:
- mel_audio: bfloat16 [128, 80, 2048], P('dp'), may hold values from -6 to 6
- start_noise: bfloat16 [128, 80, 1024], P('dp'), may hold values from -6 to 6
- span_start: int32 [128], replicated, may hold values from 0 to 2047, as said below
- span_length: int32 [128], replicated, may hold values from 1 to 1024, as said below
- block_route: int32 [512], replicated, may hold values from -1 to 191, as said below
- w_input: bfloat16 [160, 1024], replicated, may hold values from -0.5 to 0.5
- attn_gain: float32 [1024], replicated, may hold values from 0.1 to 1.9
- w_qkv: bfloat16 [1024, 3, 1024], P(None, None, 'mp'), may hold values from -4 to 4, as said below
- w_out: bfloat16 [1024, 1024], P('mp'), may hold values from -0.1875 to 0.1875
- final_gain: float32 [1024], replicated, may hold values from 0.1 to 1.9
- w_mel: bfloat16 [80, 1024], replicated, may hold values from -0.1875 to 0.1875
Outputs:
- infilled: float32 [128, 80, 1024], P('dp')
- worker_velocity: float32 [192, 80, 256], P('dp')
The draws below stay inside these ranges and needn't reach their ends.
Inputs may be any that keep to these rules, and one draw needn't show every extreme that they name: Each span lies inside its utterance: span_start[u] + span_length[u] <= 2048. `span_length`: the spans cover 192 blocks of 256 frames in all (the last block of a span may be partly filled). `block_route`: live block slots name worker slots w * 6 + j of worker w, each worker slot exactly once; empty slots hold -1. No worker receives more than 1 block from the utterances of one dp index (utterances u with the same u // 4), and some worker receives exactly 1 from one. `w_qkv`: Query, key and value projections in that order along the middle dimension.
All inputs are finite; a program needn't handle non-finite values.
Results may differ from the reference program's by a relative error of at most 0.025.
Values may be sent and summed in bfloat16 or wider, within the bound.
No kernel may reach another device: no remote copies, remote signals or barrier semaphores. Data moves between devices by JAX's collectives and lax.ppermute only.
A program may use at most 128 MiB of HBM per device.

```python
import math
import jax
import jax.numpy as jnp
from jax import lax

D = 1024
HEADS = 16
MEL = 80
HEAD_DIM = 64
BLOCK = 256
CTX = 128
BLK_UTT = 4
UTT_DEV = 4
WORK_DEV = 6
EULER = 2
FRAMES = 2048
WIN = 512
SPAN_MAX = 1024
UTTS = 128
SLOTS_ALL = 512
WORK_ALL = 192
N_MP = 4


def span_plan(key):
    split_keys = jax.random.split(jax.random.fold_in(key, 4111), 5)
    spare_blocks = BLK_UTT - 1
    cell_count = UTTS * spare_blocks
    extra_blocks = WORK_ALL - UTTS
    worker_count = WORK_ALL // WORK_DEV
    shuffled = jax.random.permutation(split_keys[0], cell_count)
    cell_rank = jnp.argsort(shuffled, stable=True).astype(jnp.int32)
    chosen = jax.random.randint(split_keys[1], (), 0, UTTS)
    cell_ids = jnp.arange(cell_count, dtype=jnp.int32)
    forced = cell_ids // spare_blocks // UTT_DEV == chosen // UTT_DEV
    cell_score = jnp.where(forced, cell_ids - cell_count, cell_rank)
    placing = jnp.argsort(jnp.argsort(cell_score, stable=True), stable=True)
    taken_mask = (placing < extra_blocks).astype(jnp.int32)
    counts = 1 + jnp.sum(taken_mask.reshape(UTTS, spare_blocks), axis=1)
    remainder = jax.random.randint(split_keys[2], (UTTS,), 1, BLOCK + 1)
    remainder = jnp.where(jnp.arange(UTTS) == chosen, BLOCK, remainder)
    length = (counts - 1) * BLOCK + remainder
    first_frame = jax.random.randint(split_keys[3], (UTTS,), 0, FRAMES - length + 1)
    live_slots = (jnp.arange(BLK_UTT)[None, :] < counts[:, None]).reshape(-1).astype(jnp.int32)
    live_order = jnp.cumsum(live_slots) - live_slots
    workers = jax.random.permutation(split_keys[4], worker_count)
    worker = workers[live_order % worker_count]
    route_table = jnp.where(live_slots > 0, worker * WORK_DEV + live_order // worker_count, -1)
    return (first_frame.astype(jnp.int32), length.astype(jnp.int32), route_table.astype(jnp.int32))


def draw_span_start(key, part):
    return span_plan(key)[0]


def draw_span_length(key, part):
    return span_plan(key)[1]


def draw_block_route(key, part):
    return span_plan(key)[2]


def draw_w_qkv(key, part):
    split_keys = jax.random.split(jax.random.fold_in(key, 977), 1)
    scale = 1.0 / math.sqrt(D)
    drawn = jnp.clip(jax.random.normal(split_keys[0], (D, 3, D)), -6.0, 6.0) * scale
    return drawn.astype(jnp.bfloat16)


def level_of(own_key, shape, pieces, smallest, largest):
    def one(dim, shards_of):
        steps = jax.random.uniform(jax.random.fold_in(jax.random.fold_in(own_key, 6), dim), (shards_of,), jnp.float32, smallest / len(pieces), largest / len(pieces))
        return jnp.repeat(jnp.exp(steps), shape[dim] // shards_of).reshape((-1,) + (1,) * (len(shape) - dim - 1))

    loudness = one(*pieces[0])
    for cut in pieces[1:]:
        loudness = loudness * one(*cut)
    return loudness


def scatter_about(key, extent, scale, limit, cuts=(), held_as=jnp.bfloat16):
    level = level_of(key, extent, cuts, -0.22, 0.18) if cuts else 1.0
    array = jax.random.normal(key, extent, jnp.float32) * scale * level
    return jnp.minimum(jnp.maximum(array, -limit), limit).astype(held_as)


def setup_inputs(seed: int = 0) -> dict:
    arg_keys = jax.random.split(jax.random.key(seed), 12)
    return {
        "mel_audio": scatter_about(arg_keys[0], (UTTS, MEL, FRAMES), 1.0, 6.0, ((0, 32),)),
        "start_noise": scatter_about(arg_keys[1], (UTTS, MEL, SPAN_MAX), 1.0, 6.0, ((0, 32),)),
        "span_start": draw_span_start(jax.random.fold_in(arg_keys[11], 71), 0),
        "span_length": draw_span_length(jax.random.fold_in(arg_keys[11], 71), 0),
        "block_route": draw_block_route(jax.random.fold_in(arg_keys[11], 71), 0),
        "w_input": scatter_about(arg_keys[5], (2 * MEL, D), (2 * MEL) ** -0.5, 0.5),
        "attn_gain": jnp.clip(1.0 + 0.18 * jax.random.normal(arg_keys[6], (D,), jnp.float32), 0.1, 1.9),
        "w_qkv": draw_w_qkv(jax.random.fold_in(arg_keys[11], 71), 0),
        "w_out": scatter_about(arg_keys[8], (D, D), D ** -0.5, 0.1875, ((0, 4),)),
        "final_gain": jnp.clip(1.0 + 0.18 * jax.random.normal(arg_keys[9], (D,), jnp.float32), 0.1, 1.9),
        "w_mel": scatter_about(arg_keys[10], (MEL, D), D ** -0.5, 0.1875),
    }


flow_steps = 32.0
norm_eps = 1e-05

def time_embed(t_value, feature_width):
    half_width = feature_width // 2
    freqs = jnp.exp(-math.log(10000.0) * jnp.arange(half_width, dtype=jnp.float32) / half_width)
    angles = 1000.0 * t_value * freqs
    return jnp.concatenate([jnp.sin(angles), jnp.cos(angles)])

def layer_norm(hidden, norm_gain):
    mean_value = lax.optimization_barrier(jnp.mean(hidden, axis=-1, keepdims=True))
    centred = hidden - mean_value
    variance = lax.optimization_barrier(jnp.mean(centred * centred, axis=-1, keepdims=True))
    return centred * lax.rsqrt(variance + norm_eps) * norm_gain.astype(jnp.float32)

def velocity(window, window_begin, own_count, t_value, w_input, attn_gain, w_qkv, w_out, final_gain, w_mel):
    hidden = jnp.dot(window.T, w_input, preferred_element_type=jnp.float32)
    hidden = hidden + time_embed(t_value, D)[None, :]
    normed = layer_norm(hidden, attn_gain).astype(jnp.bfloat16)
    queries = jnp.dot(normed[CTX:CTX + BLOCK], w_qkv[:, 0, :], preferred_element_type=jnp.float32).astype(jnp.bfloat16)
    key_rows = jnp.dot(normed, w_qkv[:, 1, :], preferred_element_type=jnp.float32).astype(jnp.bfloat16)
    value_rows = jnp.dot(normed, w_qkv[:, 2, :], preferred_element_type=jnp.float32).astype(jnp.bfloat16)
    query_heads = queries.astype(jnp.float32).reshape(BLOCK, HEADS, HEAD_DIM)
    key_heads = key_rows.astype(jnp.float32).reshape(WIN, HEADS, HEAD_DIM)
    value_heads = value_rows.astype(jnp.float32).reshape(WIN, HEADS, HEAD_DIM)
    scores = jnp.einsum('qhd,khd->hqk', query_heads, key_heads) * (1.0 / math.sqrt(HEAD_DIM))
    position = window_begin - CTX + jnp.arange(WIN, dtype=jnp.int32)
    usable = (position >= 0) & (position < FRAMES)
    scores = jnp.where(usable[None, None, :], scores, -1e+30)
    attn_weights = jax.nn.softmax(scores, axis=-1).astype(jnp.bfloat16)
    head_outputs = jnp.einsum('hqk,khd->qhd', attn_weights.astype(jnp.float32), value_heads)
    head_outputs = head_outputs.astype(jnp.bfloat16).reshape(BLOCK, D)
    group_width = D // N_MP
    attended = jnp.zeros((BLOCK, D), jnp.float32)
    for mp_part in range(N_MP):
        lower = mp_part * group_width
        term = jnp.dot(head_outputs[:, lower:lower + group_width], w_out[lower:lower + group_width], preferred_element_type=jnp.float32)
        attended = attended + term.astype(jnp.bfloat16).astype(jnp.float32)
    final = layer_norm(hidden[CTX:CTX + BLOCK] + attended, final_gain).astype(jnp.bfloat16)
    result = jnp.dot(w_mel, final.T, preferred_element_type=jnp.float32)
    live_mask = jnp.arange(BLOCK, dtype=jnp.int32) < own_count
    return jnp.where(live_mask[None, :], result, 0.0)

def reference(mel_audio, start_noise, span_start, span_length, block_route, w_input, attn_gain, w_qkv, w_out, final_gain, w_mel):
    slot_ids = jnp.arange(WORK_ALL, dtype=jnp.int32)
    every_slot = jnp.arange(SLOTS_ALL, dtype=jnp.int32)
    matches = block_route[None, :] == slot_ids[:, None]
    blocks = lax.optimization_barrier(jnp.sum(jnp.where(matches, every_slot[None, :], 0), axis=1)).astype(jnp.int32)
    padded = jnp.pad(mel_audio, ((0, 0), (0, 0), (CTX, SPAN_MAX + CTX)))
    zero_index = jnp.zeros((), jnp.int32)

    def solve_block(block_index):
        utterance = (block_index // BLK_UTT).astype(jnp.int32)
        block_order = (block_index % BLK_UTT).astype(jnp.int32)
        first_frame = span_start[utterance]
        length = span_length[utterance]
        window_begin = (first_frame + BLOCK * block_order).astype(jnp.int32)
        audio_rows = lax.dynamic_slice(padded, (utterance, zero_index, window_begin), (1, MEL, WIN))[0]
        position = window_begin - CTX + jnp.arange(WIN, dtype=jnp.int32)
        in_span = (position >= first_frame) & (position < first_frame + length)
        context = jnp.where(in_span[None, :], jnp.zeros((), jnp.bfloat16), audio_rows)
        own_count = jnp.minimum(BLOCK, length - BLOCK * block_order)
        live_mask = jnp.arange(BLOCK, dtype=jnp.int32) < own_count
        frames_state = lax.dynamic_slice(start_noise, (utterance, zero_index, (BLOCK * block_order).astype(jnp.int32)), (1, MEL, BLOCK))[0].astype(jnp.float32)
        side_zeros = jnp.zeros((MEL, CTX), jnp.bfloat16)
        result = jnp.zeros((MEL, BLOCK), jnp.float32)
        total = jnp.zeros((MEL, BLOCK), jnp.float32)
        for euler_step in range(EULER):
            state_rows = jnp.where(live_mask[None, :], frames_state, 0.0).astype(jnp.bfloat16)
            state_window = jnp.concatenate([side_zeros, state_rows, side_zeros], axis=1)
            window = jnp.concatenate([context, state_window], axis=0)
            result = velocity(window, window_begin, own_count, euler_step / flow_steps, w_input, attn_gain, w_qkv, w_out, final_gain, w_mel)
            frames_state = frames_state + result * (1.0 / flow_steps)
            total = total + result
        return (result, jnp.where(live_mask[None, :], total, 0.0))
    worker_velocity, finals = lax.map(solve_block, blocks)
    slotted = jnp.zeros((SLOTS_ALL, MEL, BLOCK), jnp.float32).at[blocks].set(finals)
    infilled = slotted.reshape(UTTS, BLK_UTT, MEL, BLOCK).transpose(0, 2, 1, 3).reshape(UTTS, MEL, SPAN_MAX)
    return (infilled, worker_velocity)
```

```python
import math

import jax
import jax.numpy as jnp
import numpy as np
from jax import lax
from jax.experimental import pallas as pl
from jax.experimental.pallas import tpu as pltpu
from jax.sharding import PartitionSpec as P

D = 1024
MEL = 80
HEAD_DIM = 64
HEADS = 16
BLOCK = 256
CTX = 128
BLK_UTT = 4
UTT_DEV = 4
WORK_DEV = 6
EULER = 2
FRAMES = 2048
WIN = 512
SPAN_MAX = 1024
SLOT_DEV = 16
N_MP = 4
JOBS = 4
ROWS = 176
PIECE = 48
flow_steps = 32.0
norm_eps = 1e-05
f32 = jnp.float32
bf16 = jnp.bfloat16
VMEM = pltpu.VMEM
SMEM = pltpu.SMEM
LIMIT = 56 * 1024 * 1024


def time_rows():
    half = D // 2
    freqs = np.exp(-math.log(10000.0) * np.arange(half, dtype=np.float32) / half)
    rows = np.zeros((16, D), np.float32)
    for step in range(EULER):
        angles = np.float32(1000.0 * step / flow_steps) * freqs.astype(np.float32)
        e = np.concatenate([np.sin(angles), np.cos(angles)])
        e = e - e.mean()
        rows[2 * step] = e
        rows[2 * step + 1] = e
    return rows


def high_low(rows):
    high = rows.astype(bf16).astype(f32)
    odd = lax.broadcasted_iota(jnp.int32, rows.shape, 0) % 2 == 1
    return jnp.where(odd, rows - high, high)


def fold_kernel(w_in, e_rows, gain, w_qkv, out):
    w = w_in[...].astype(f32)
    wc = w - jnp.mean(w, axis=1, keepdims=True)
    g = gain[...]
    wag = jnp.concatenate([wc * g, high_low(e_rows[...] * g)], axis=0).astype(bf16)
    for c in range(3):
        res = jnp.dot(wag, w_qkv[c], preferred_element_type=f32)
        if c == 0:
            res = res * (math.log2(math.e) / math.sqrt(HEAD_DIM))
        e_res = res[160:176]
        row = lax.broadcasted_iota(jnp.int32, e_res.shape, 0)
        first = e_res[0:1] + e_res[1:2]
        second = e_res[2:3] + e_res[3:4]
        both = jnp.where(row < 2, first, jnp.where(row < 4, second, 0.0))
        out[c, 0:160, :] = res[0:160].astype(bf16)
        out[c, 160:176, :] = high_low(both).astype(bf16)


def prep_kernel(w_in, e_rows, w_out, w_mel, gain, wa_t, wo_t, wm):
    w = w_in[...].astype(f32)
    wc = w - jnp.mean(w, axis=1, keepdims=True)
    wa = jnp.concatenate([wc, high_low(e_rows[...]), jnp.zeros((80, D), f32)], axis=0)
    wa_t[...] = wa.T[:, :ROWS].astype(bf16)
    wo_t[...] = w_out[...].astype(f32).T.astype(bf16)
    m = w_mel[...].astype(f32) * gain[...]
    high = m.astype(bf16)
    wm[0:MEL, :] = high
    wm[MEL : 2 * MEL, :] = (m - high.astype(f32)).astype(bf16)


def main_kernel(
    ids, route, starts, lengths, mel, noise, wa_t, wm,
    wp0, wp1, wp2, wp3, wo0, wo1, wo2, wo3,
    tot_out, v0, v1, v2, v3,
    job_smem, wq_s, wv_s, wk_s, wr_s, win_s, ws_s, wst_s, q_s, k_s, v_s, o_s, x_s, tot_s, stage,
):
    me = ids[0]
    m = ids[1]

    def scan(s, rank):
        dest = route[me * SLOT_DEV + s]
        live = dest >= 0
        mine = jnp.logical_and(live, (rank & 3) == m)

        @pl.when(mine)
        def _():
            job_smem[rank >> 2] = s

        return rank + live.astype(jnp.int32)

    n_live = lax.fori_loop(0, SLOT_DEV, scan, jnp.int32(0))
    n_jobs = (n_live - m + 3) >> 2

    for k, (wp, wo) in enumerate(zip((wp0, wp1, wp2, wp3), (wo0, wo1, wo2, wo3))):
        lanes = slice(256 * k, 256 * k + 256)
        pad = jnp.zeros((256 - ROWS, 256), f32)
        wq_s[lanes, :] = jnp.concatenate([wp[0].astype(f32), pad], axis=0).T.astype(bf16)[:, :ROWS]
        wv_s[lanes, :] = jnp.concatenate([wp[2].astype(f32), pad], axis=0).T.astype(bf16)[:, :ROWS]
        wk_s[:, lanes] = wp[1]
        wr_s[:, lanes] = wo[...]
    wr_s[:, 1024 : 1024 + ROWS] = wa_t[...]

    def job(q, carry):
        s = job_smem[q]
        u = s >> 2
        order = s & 3
        span = starts[me * UTT_DEV + u]
        length = lengths[me * UTT_DEV + u]
        begin = span + BLOCK * order
        count = jnp.minimum(BLOCK, length - BLOCK * order)
        first = begin - CTX
        aligned = jnp.clip((first >> 7) << 7, 0, FRAMES - 640)
        aligned = pl.multiple_of(aligned, 128)
        chunk = mel[u, :, pl.ds(aligned, 640)].astype(f32)
        shift = aligned - first
        shift = jnp.where(shift < 0, shift + 640, shift)
        chunk = pltpu.roll(chunk, shift, 1)[:, :WIN]
        pos = first + lax.broadcasted_iota(jnp.int32, (1, WIN), 1)
        valid = jnp.logical_and(pos >= 0, pos < FRAMES)
        in_span = jnp.logical_and(pos >= span, pos < span + length)
        keep = jnp.logical_and(valid, jnp.logical_not(in_span))
        context = jnp.where(keep, chunk, 0.0)
        own = lax.broadcasted_iota(jnp.int32, (1, BLOCK), 1) < count
        off = pl.multiple_of(order * BLOCK, BLOCK)
        x_s[...] = jnp.where(own, noise[u, :, pl.ds(off, BLOCK)].astype(f32), 0.0)
        tot_s[...] = jnp.zeros((MEL, BLOCK), f32)
        valid_f = valid.astype(f32)
        ones_rows = jnp.broadcast_to(valid_f, (16, WIN)).astype(bf16)

        def step(n, c2):
            xr = x_s[...].astype(bf16).astype(f32)
            side = jnp.zeros((MEL, CTX), f32)
            state = jnp.concatenate([side, xr, side], axis=1)
            flags = (lax.broadcasted_iota(jnp.int32, (16, WIN), 0) >> 1) == n
            win = jnp.concatenate([context, state, flags.astype(f32)], axis=0)
            win = jnp.where(valid, win, win[:, CTX : CTX + 1])
            win_b = win.astype(bf16)
            win_s[...] = win_b
            o_s[1024 : 1024 + ROWS, :] = win_b[:, CTX : CTX + BLOCK]
            hid = jnp.dot(wa_t[...], win_b, preferred_element_type=f32)
            var = jnp.sum(hid * hid, axis=0, keepdims=True) * (1.0 / D)
            rstd = lax.rsqrt(var + norm_eps)
            scaled = win * rstd
            ws_s[...] = scaled.astype(bf16)
            padded = jnp.concatenate([scaled, jnp.zeros((256 - ROWS, WIN), f32)], axis=0)
            wst_s[...] = padded.T.astype(bf16)[:, :ROWS]
            q_s[...] = jnp.dot(
                wq_s[...], ws_s[:, CTX : CTX + BLOCK], preferred_element_type=f32
            ).astype(bf16)
            v_win = (scaled * valid_f).astype(bf16)
            v_s[...] = jnp.dot(wv_s[...], v_win, preferred_element_type=f32).astype(bf16)
            keys = jnp.dot(wst_s[...], wk_s[...], preferred_element_type=f32).astype(bf16)
            for p in range(HEADS // 2):
                k_s[p] = keys[:, 128 * p : 128 * p + 128]

            def heads(g, c3):
                for pp in range(2):
                    p = g * 2 + pp
                    kp = k_s[p]
                    base = pl.multiple_of(p * 128, 128)
                    qp = q_s[pl.ds(base, 128), :]
                    zero = jnp.zeros((HEAD_DIM, BLOCK), bf16)
                    for j in range(2):
                        qh = qp[64 * j : 64 * j + 64]
                        qz = jnp.concatenate([qh, zero] if j == 0 else [zero, qh], axis=0)
                        sc = jnp.dot(kp, qz, preferred_element_type=f32)
                        top = jnp.max(sc, axis=0, keepdims=True)
                        pr = jnp.exp2(sc - top).astype(bf16)
                        vh = v_s[pl.ds(pl.multiple_of(base + 64 * j, 64), 64), :]
                        lhs = jnp.concatenate([vh, ones_rows], axis=0)
                        ov = jnp.dot(lhs, pr, preferred_element_type=f32)
                        o = ov[0:64] / ov[64:65]
                        o_s[pl.ds(pl.multiple_of(base + 64 * j, 64), 64), :] = o.astype(bf16)
                return c3

            lax.fori_loop(0, HEADS // 4, heads, 0)
            r = jnp.dot(wr_s[...], o_s[...], preferred_element_type=f32)
            mean = jnp.sum(r, axis=0, keepdims=True) * (1.0 / D)
            rc = r - mean
            rvar = jnp.sum(rc * rc, axis=0, keepdims=True) * (1.0 / D)
            vv = jnp.dot(wm[...], rc.astype(bf16), preferred_element_type=f32)
            vel = (vv[0:MEL] + vv[MEL : 2 * MEL]) * lax.rsqrt(rvar + norm_eps)
            vel = jnp.where(own, vel, 0.0)
            x_s[...] = x_s[...] + vel * (1.0 / flow_steps)
            tot_s[...] = tot_s[...] + vel
            velb = vel.astype(bf16)
            stage[0:MEL, :] = velb[:, 0:128]
            stage[MEL : 2 * MEL, :] = velb[:, 128:256]
            return c2

        lax.fori_loop(0, EULER, step, 0)
        totb = tot_s[...].astype(bf16)
        tot_out[q, 0:MEL, :] = totb[:, 0:128]
        tot_out[q, MEL : 2 * MEL, :] = totb[:, 128:256]
        for k, out in enumerate((v0, v1, v2, v3)):
            quarter = (m + k) & 3
            out[q] = stage[pl.ds(pl.multiple_of(quarter * PIECE, 16), PIECE), :]
        return carry

    stage[...] = jnp.zeros(stage.shape, bf16)
    lax.fori_loop(0, n_jobs, job, 0)


def pack_kernel(ids, route, a0, a1, a2, a3, out):
    me = ids[0]
    m = ids[1]

    def scan(s, rank):
        dest = route[me * SLOT_DEV + s]
        live = dest >= 0
        worker = (jnp.maximum(dest, 0) * 10923) >> 16
        source = (m - rank) & 3
        for k, a in enumerate((a0, a1, a2, a3)):

            @pl.when(jnp.logical_and(live, source == k))
            def _():
                out[worker] = a[rank >> 2]

        return rank + live.astype(jnp.int32)

    lax.fori_loop(0, SLOT_DEV, scan, jnp.int32(0))


def select_kernel(owners, got, out):
    for j in range(WORK_DEV):
        out[j] = got[owners[j]]


def span_kernel(ids, route, t0, t1, t2, t3, out):
    me = ids[0]
    m = ids[1]
    out[...] = jnp.zeros(out.shape, f32)

    def scan(s, rank):
        live = route[me * SLOT_DEV + s] >= 0
        source = (m - rank) & 3
        u = s >> 2
        off = (s & 3) * BLOCK
        for k, t in enumerate((t0, t1, t2, t3)):

            @pl.when(jnp.logical_and(live, source == k))
            def _():
                block = t[rank >> 2].astype(f32)
                out[u, :, pl.ds(pl.multiple_of(off, 128), 128)] = block[0:MEL]
                out[u, :, pl.ds(pl.multiple_of(off + 128, 128), 128)] = block[MEL : 2 * MEL]

        return rank + live.astype(jnp.int32)

    lax.fori_loop(0, SLOT_DEV, scan, jnp.int32(0))


def final_kernel(ids, b0, b1, b2, b3, out, stage):
    m = ids[1]
    for k, b in enumerate((b0, b1, b2, b3)):
        quarter = (m - k) & 3
        at = pl.multiple_of(quarter * PIECE, 16)
        for j in range(WORK_DEV):
            stage[j, pl.ds(at, PIECE), :] = b[j]
    for j in range(WORK_DEV):
        out[j, :, 0:128] = stage[j, 0:MEL, :].astype(f32)
        out[j, :, 128:256] = stage[j, MEL : 2 * MEL, :].astype(f32)


def call(kernel, outs, kinds, args, scratch=(), out_kinds=None):
    spec = lambda kind: pl.BlockSpec(memory_space=SMEM if kind == "s" else VMEM)
    return pl.pallas_call(
        kernel,
        out_shape=outs,
        in_specs=[spec(k) for k in kinds],
        out_specs=jax.tree.map(lambda _: pl.BlockSpec(memory_space=VMEM), outs),
        scratch_shapes=list(scratch),
        compiler_params=pltpu.CompilerParams(vmem_limit_bytes=LIMIT),
    )(*args)


def shape(dims, dtype):
    return jax.ShapeDtypeStruct(dims, dtype)


def to_next(value, k):
    return lax.ppermute(value, "mp", [(i, (i + k) % N_MP) for i in range(N_MP)])


def gathered(value):
    return [value] + [to_next(value, k) for k in range(1, N_MP)]


def shards(
    mel_audio, start_noise, span_start, span_length, block_route,
    w_input, attn_gain, w_qkv, w_out, final_gain, w_mel,
):
    e_rows = jnp.asarray(time_rows())
    gain = attn_gain.reshape(1, D)
    w3 = jnp.transpose(w_qkv, (1, 0, 2))
    folded = call(fold_kernel, shape((3, ROWS, 256), bf16), "vvvv", (w_input, e_rows, gain, w3))
    wp = gathered(folded)
    wa_t, wo_t, wm = call(
        prep_kernel,
        (shape((D, ROWS), bf16), shape((D, 256), bf16), shape((2 * MEL, D), bf16)),
        "vvvvv",
        (w_input, e_rows, w_out, w_mel, final_gain.reshape(1, D)),
    )
    wo = gathered(wo_t)
    ids = jnp.stack([lax.axis_index("dp"), lax.axis_index("mp")]).astype(jnp.int32)
    slot_ids = ids[0] * WORK_DEV + jnp.arange(WORK_DEV, dtype=jnp.int32)
    matches = block_route[None, :] == slot_ids[:, None]
    every = jnp.arange(block_route.shape[0], dtype=jnp.int32)
    owners = jnp.sum(jnp.where(matches, every[None, :], 0), axis=1) // SLOT_DEV

    tot, v0, v1, v2, v3 = call(
        main_kernel,
        (shape((JOBS, 2 * MEL, 128), bf16),) + (shape((JOBS, PIECE, 128), bf16),) * 4,
        "ssss" + "v" * 12,
        (ids, block_route, span_start, span_length, mel_audio, start_noise, wa_t, wm, *wp, *wo),
        scratch=[
            SMEM((JOBS,), jnp.int32),
            VMEM((D, ROWS), bf16),
            VMEM((D, ROWS), bf16),
            VMEM((ROWS, D), bf16),
            VMEM((D, D + ROWS), bf16),
            VMEM((ROWS, WIN), bf16),
            VMEM((ROWS, WIN), bf16),
            VMEM((WIN, ROWS), bf16),
            VMEM((D, BLOCK), bf16),
            VMEM((HEADS // 2, WIN, 128), bf16),
            VMEM((D, WIN), bf16),
            VMEM((D + ROWS, BLOCK), bf16),
            VMEM((MEL, BLOCK), f32),
            VMEM((MEL, BLOCK), f32),
            VMEM((4 * PIECE, 128), bf16),
        ],
    )
    pieces = [v0] + [to_next(v, k) for k, v in ((1, v1), (2, v2), (3, v3))]
    totals = gathered(tot)
    packed = call(
        pack_kernel, shape((32, PIECE, 128), bf16), "ssvvvv", (ids, block_route, *pieces)
    )
    got = lax.all_to_all(packed, "dp", 0, 0, tiled=True)
    chosen = call(select_kernel, shape((WORK_DEV, PIECE, 128), bf16), "sv", (owners, got))
    parts = gathered(chosen)
    infilled = call(
        span_kernel, shape((UTT_DEV, MEL, SPAN_MAX), f32), "ssvvvv", (ids, block_route, *totals)
    )
    velocity = call(
        final_kernel,
        shape((WORK_DEV, MEL, BLOCK), f32),
        "svvvv",
        (ids, *parts),
        scratch=[VMEM((WORK_DEV, 4 * PIECE, 128), bf16)],
    )
    return (infilled, velocity)


def solution(mesh):
    return jax.shard_map(
        shards,
        mesh=mesh,
        in_specs=(
            P("dp", None, None),
            P("dp", None, None),
            P(),
            P(),
            P(),
            P(),
            P(),
            P(None, None, "mp"),
            P("mp", None),
            P(),
            P(),
        ),
        out_specs=(P("dp", None, None), P("dp", None, None)),
        check_vma=False,
    )
```

```python
import math

import jax
import jax.numpy as jnp
import numpy as np
from jax import lax
from jax.experimental import pallas as pl
from jax.experimental.pallas import tpu as pltpu
from jax.sharding import PartitionSpec as P

D = 1024
MEL = 80
HEAD_DIM = 64
HEADS = 16
BLOCK = 256
CTX = 128
BLK_UTT = 4
UTT_DEV = 4
WORK_DEV = 6
EULER = 2
FRAMES = 2048
WIN = 512
SPAN_MAX = 1024
SLOT_DEV = 16
N_MP = 4
JOBS = 4
ROWS = 176
PIECE = 48
flow_steps = 32.0
norm_eps = 1e-05
f32 = jnp.float32
bf16 = jnp.bfloat16
VMEM = pltpu.VMEM
SMEM = pltpu.SMEM
LIMIT = 56 * 1024 * 1024


def time_rows():
    half = D // 2
    freqs = np.exp(-math.log(10000.0) * np.arange(half, dtype=np.float32) / half)
    rows = np.zeros((16, D), np.float32)
    for step in range(EULER):
        angles = np.float32(1000.0 * step / flow_steps) * freqs.astype(np.float32)
        e = np.concatenate([np.sin(angles), np.cos(angles)])
        e = e - e.mean()
        rows[2 * step] = e
        rows[2 * step + 1] = e
    return rows


def high_low(rows):
    high = rows.astype(bf16).astype(f32)
    odd = lax.broadcasted_iota(jnp.int32, rows.shape, 0) % 2 == 1
    return jnp.where(odd, rows - high, high)


def fold_kernel(ids, w_in, e_rows, gain, w_qkv, out, half):
    w = w_in[...].astype(f32)
    wc = w - jnp.mean(w, axis=1, keepdims=True)
    g = gain[...]
    wag = jnp.concatenate([wc * g, high_low(e_rows[...] * g)], axis=0).astype(bf16)
    for c in range(3):
        res = jnp.dot(wag, w_qkv[c], preferred_element_type=f32)
        if c == 0:
            res = res * (math.log2(math.e) / math.sqrt(HEAD_DIM))
        e_res = res[160:176]
        row = lax.broadcasted_iota(jnp.int32, e_res.shape, 0)
        first = e_res[0:1] + e_res[1:2]
        second = e_res[2:3] + e_res[3:4]
        both = jnp.where(row < 2, first, jnp.where(row < 4, second, 0.0))
        out[c, 0:160, :] = res[0:160].astype(bf16)
        out[c, 160:176, :] = high_low(both).astype(bf16)
        half[c] = jnp.where((ids[0] & 1) == 0, out[c, :, 0:128], out[c, :, 128:256])


def prep_kernel(ids, w_in, e_rows, w_out, w_mel, gain, wa_t, gram, wo_t, half, wm):
    w = w_in[...].astype(f32)
    wc = w - jnp.mean(w, axis=1, keepdims=True)
    wa = jnp.concatenate([wc, high_low(e_rows[...]), jnp.zeros((80, D), f32)], axis=0)
    wa_t[...] = wa.T[:, :ROWS].astype(bf16)
    wab = wa.astype(bf16)
    g = lax.dot_general(wab, wab, (((1,), (1,)), ((), ())), preferred_element_type=f32)
    g = g[0:ROWS, 0:ROWS] * (1.0 / D)
    high = g.astype(bf16)
    gram[0:ROWS, :] = high
    gram[ROWS : 2 * ROWS, :] = (g - high.astype(f32)).astype(bf16)
    o = w_out[...].astype(f32)
    o = o - jnp.mean(o, axis=1, keepdims=True)
    wo_t[...] = o.T.astype(bf16)
    half[...] = jnp.where((ids[0] & 1) == 0, wo_t[:, 0:128], wo_t[:, 128:256])
    wm[...] = (w_mel[...].astype(f32) * gain[...]).astype(bf16)


def find_jobs(ids, route, job_smem):
    base = (ids[0] >> 1) * (2 * SLOT_DEV)
    seat = (ids[0] & 1) * N_MP + ids[1]

    def scan(s, rank):
        live = route[base + s] >= 0

        @pl.when(jnp.logical_and(live, (rank & 7) == seat))
        def _():
            job_smem[rank >> 3] = s

        return rank + live.astype(jnp.int32)

    n_live = lax.fori_loop(0, 2 * SLOT_DEV, scan, jnp.int32(0))
    return (n_live - seat + 7) >> 3


def place(ids, starts, lengths, s):
    u = (s >> 2) & 3
    order = s & 3
    utter = (ids[0] >> 1) * (2 * UTT_DEV) + (s >> 2)
    span = starts[utter]
    length = lengths[utter]
    return u, order, span, length


def own_mask(order, length):
    count = length - BLOCK * order
    return lax.broadcasted_iota(jnp.int32, (1, BLOCK), 1) < count


def load_context(ids, s, u, order, span, length, mel_a, mel_b, chunk_s):
    first = span + BLOCK * order - CTX
    aligned = pl.multiple_of(jnp.clip((first >> 7) << 7, 0, FRAMES - 640), 128)
    here = (s >> 4) == (ids[0] & 1)

    @pl.when(here)
    def _():
        chunk_s[...] = mel_a[u, :, pl.ds(aligned, 640)]

    @pl.when(jnp.logical_not(here))
    def _():
        chunk_s[...] = mel_b[u, :, pl.ds(aligned, 640)]

    shift = aligned - first
    shift = jnp.where(shift < 0, shift + 640, shift)
    chunk = pltpu.roll(chunk_s[...].astype(f32), shift, 1)[:, :WIN]
    pos = first + lax.broadcasted_iota(jnp.int32, (1, WIN), 1)
    valid = jnp.logical_and(pos >= 0, pos < FRAMES)
    in_span = jnp.logical_and(pos >= span, pos < span + length)
    keep = jnp.logical_and(valid, jnp.logical_not(in_span))
    return jnp.where(keep, chunk, 0.0), valid.astype(f32)


def load_noise(ids, s, u, order, own, noise_a, noise_b, x_s):
    off = pl.multiple_of(order * BLOCK, BLOCK)
    here = (s >> 4) == (ids[0] & 1)

    @pl.when(here)
    def _():
        x_s[...] = jnp.where(own, noise_a[u, :, pl.ds(off, BLOCK)].astype(f32), 0.0)

    @pl.when(jnp.logical_not(here))
    def _():
        x_s[...] = jnp.where(own, noise_b[u, :, pl.ds(off, BLOCK)].astype(f32), 0.0)


def attend(n, context, valid, x, weights, work, o_out):
    gram, wq_s, wv_s, wk_s = weights
    k_s, q_s, v_s = work
    xr = x.astype(bf16).astype(f32)
    side = jnp.zeros((MEL, CTX), f32)
    state = jnp.concatenate([side, xr, side], axis=1)
    flags = (lax.broadcasted_iota(jnp.int32, (16, WIN), 0) >> 1) == n
    win = jnp.concatenate([context, state, flags.astype(f32)], axis=0)
    win = jnp.where(valid > 0.0, win, win[:, CTX : CTX + 1])
    win_b = win.astype(bf16)
    o_out[1024 : 1024 + ROWS, :] = win_b[:, CTX : CTX + BLOCK]
    gw = jnp.dot(gram[...], win_b, preferred_element_type=f32)
    var = jnp.sum(win * (gw[0:ROWS] + gw[ROWS : 2 * ROWS]), axis=0, keepdims=True)
    rstd = lax.rsqrt(jnp.maximum(var, 0.0) + norm_eps)
    scaled = win * rstd
    scaled_b = scaled.astype(bf16)
    v_win = (scaled * valid).astype(bf16)
    padded = jnp.concatenate([scaled, jnp.zeros((256 - ROWS, WIN), f32)], axis=0)
    win_t = padded.T.astype(bf16)[:, :ROWS]
    q_s[...] = jnp.dot(
        wq_s[...], scaled_b[:, CTX : CTX + BLOCK], preferred_element_type=f32
    ).astype(bf16)
    keys = jnp.dot(win_t, wk_s[...], preferred_element_type=f32).astype(bf16)
    for p in range(4):
        k_s[p] = keys[:, 256 * p : 256 * p + 256]
    v_s[...] = jnp.dot(wv_s[...], v_win, preferred_element_type=f32).astype(bf16)
    ones_rows = jnp.broadcast_to(valid, (16, WIN)).astype(bf16)
    zero = jnp.zeros((HEAD_DIM, BLOCK), bf16)

    def heads(half, carry):
        for quad in range(2):
            g = half * 2 + quad
            base = pl.multiple_of(g * 256, 256)
            qq = q_s[pl.ds(base, 256), :]
            columns = []
            for j in range(4):
                rows = [qq[64 * j : 64 * j + 64] if t == j else zero for t in range(4)]
                columns.append(jnp.concatenate(rows, axis=0))
            sc = jnp.dot(k_s[g], jnp.concatenate(columns, axis=1), preferred_element_type=f32)
            top = jnp.max(sc, axis=0, keepdims=True)
            pr = jnp.exp2(sc - top).astype(bf16)
            for j in range(4):
                at = pl.multiple_of(base + 64 * j, 64)
                lhs = jnp.concatenate([v_s[pl.ds(at, 64), :], ones_rows], axis=0)
                ov = jnp.dot(lhs, pr[:, 256 * j : 256 * j + 256], preferred_element_type=f32)
                o_out[pl.ds(at, 64), :] = (ov[0:64] / ov[64:65]).astype(bf16)
        return carry

    lax.fori_loop(0, 2, heads, 0)


def velocity_of(wr_s, o, own):
    r = jnp.dot(wr_s[...], o[...], preferred_element_type=f32)
    body = r[0:D]
    var = jnp.sum(body * body, axis=0, keepdims=True) * (1.0 / D)
    return jnp.where(own, r[D : D + MEL] * lax.rsqrt(var + norm_eps), 0.0)


def first_kernel(
    ids, route, starts, lengths, mel_a, mel_b, noise_a, noise_b, gram,
    wp0, hp1, sp1, hp2, sp2, hp3, sp3,
    wq_s, wv_s, wk_s, o_out,
    job_smem, k_s, q_s, v_s, x_s, chunk_s, o_s,
):
    n_jobs = find_jobs(ids, route, job_smem)
    at = 0
    for wp in (wp0, hp1, sp1, hp2, sp2, hp3, sp3):
        width = wp.shape[2]
        lanes = slice(at, at + width)
        pad = jnp.zeros((256 - ROWS, width), f32)
        wq_s[lanes, :] = jnp.concatenate([wp[0].astype(f32), pad], axis=0).T.astype(bf16)[:, :ROWS]
        wv_s[lanes, :] = jnp.concatenate([wp[2].astype(f32), pad], axis=0).T.astype(bf16)[:, :ROWS]
        wk_s[:, lanes] = wp[1]
        at += width

    def job(q, carry):
        s = job_smem[q]
        u, order, span, length = place(ids, starts, lengths, s)
        own = own_mask(order, length)
        context, valid = load_context(ids, s, u, order, span, length, mel_a, mel_b, chunk_s)
        load_noise(ids, s, u, order, own, noise_a, noise_b, x_s)
        attend(0, context, valid, x_s[...], (gram, wq_s, wv_s, wk_s), (k_s, q_s, v_s), o_s)
        o_out[q] = o_s[...]
        return carry

    lax.fori_loop(0, n_jobs, job, 0)


def second_kernel(
    ids, route, starts, lengths, mel_a, mel_b, noise_a, noise_b, gram,
    wq_s, wv_s, wk_s, o_in, wa_t, wm,
    wo0, ho1, so1, ho2, so2, ho3, so3,
    tot_out, v0, v1, v2, v3,
    job_smem, k_s, q_s, v_s, x_s, chunk_s, o_s, wr_s, stage,
):
    m = ids[1]
    n_jobs = find_jobs(ids, route, job_smem)
    at = 0
    for wo in (wo0, ho1, so1, ho2, so2, ho3, so3):
        width = wo.shape[1]
        wr_s[0:D, at : at + width] = wo[...]
        at += width
    wr_s[0:D, 1024 : 1024 + ROWS] = wa_t[...]
    wr_s[D : D + MEL, :] = jnp.dot(wm[...], wr_s[0:D, :], preferred_element_type=f32).astype(bf16)
    stage[...] = jnp.zeros(stage.shape, bf16)

    def job(q, carry):
        s = job_smem[q]
        u, order, span, length = place(ids, starts, lengths, s)
        own = own_mask(order, length)
        context, valid = load_context(ids, s, u, order, span, length, mel_a, mel_b, chunk_s)
        load_noise(ids, s, u, order, own, noise_a, noise_b, x_s)
        first = velocity_of(wr_s, o_in.at[q], own)
        x = x_s[...] + first * (1.0 / flow_steps)
        attend(1, context, valid, x, (gram, wq_s, wv_s, wk_s), (k_s, q_s, v_s), o_s)
        last = velocity_of(wr_s, o_s, own)
        total = (first + last).astype(bf16)
        tot_out[q, 0:MEL, :] = total[:, 0:128]
        tot_out[q, MEL : 2 * MEL, :] = total[:, 128:256]
        vel = last.astype(bf16)
        stage[0:MEL, :] = vel[:, 0:128]
        stage[MEL : 2 * MEL, :] = vel[:, 128:256]
        for k, out in enumerate((v0, v1, v2, v3)):
            quarter = (m + k) & 3
            out[q] = stage[pl.ds(pl.multiple_of(quarter * PIECE, 16), PIECE), :]
        return carry

    lax.fori_loop(0, n_jobs, job, 0)


def each_own_block(ids, route, arrays, use):
    m = ids[1]
    core = ids[0] & 1
    base = (ids[0] >> 1) * (2 * SLOT_DEV)

    def scan(s, rank):
        dest = route[base + s]
        live = dest >= 0
        mine = jnp.logical_and(live, (s >> 4) == core)
        k = (m - rank) & 3
        away = ((rank >> 2) & 1) ^ core
        source = away * 4 + k
        for i, a in enumerate(arrays):

            @pl.when(jnp.logical_and(mine, source == i))
            def _():
                use(s & 15, dest, a, rank >> 3)

        return rank + live.astype(jnp.int32)

    lax.fori_loop(0, 2 * SLOT_DEV, scan, jnp.int32(0))


def pack_kernel(ids, route, a0, a1, a2, a3, b0, b1, b2, b3, out):
    def use(s, dest, a, q):
        out[(dest * 10923) >> 16] = a[q]

    each_own_block(ids, route, (a0, a1, a2, a3, b0, b1, b2, b3), use)


def select_kernel(owners, got, out):
    for j in range(WORK_DEV):
        out[j] = got[owners[j]]


def span_kernel(ids, route, a0, a1, a2, a3, b0, b1, b2, b3, out):
    out[...] = jnp.zeros(out.shape, f32)

    def use(s, dest, a, q):
        block = a[q].astype(f32)
        off = (s & 3) * BLOCK
        out[s >> 2, :, pl.ds(pl.multiple_of(off, 128), 128)] = block[0:MEL]
        out[s >> 2, :, pl.ds(pl.multiple_of(off + 128, 128), 128)] = block[MEL : 2 * MEL]

    each_own_block(ids, route, (a0, a1, a2, a3, b0, b1, b2, b3), use)


def final_kernel(ids, b0, b1, b2, b3, out, stage):
    m = ids[1]
    for k, b in enumerate((b0, b1, b2, b3)):
        quarter = (m - k) & 3
        at = pl.multiple_of(quarter * PIECE, 16)
        for j in range(WORK_DEV):
            stage[j, pl.ds(at, PIECE), :] = b[j]
    for j in range(WORK_DEV):
        out[j, :, 0:128] = stage[j, 0:MEL, :].astype(f32)
        out[j, :, 128:256] = stage[j, MEL : 2 * MEL, :].astype(f32)


def call(kernel, outs, kinds, args, scratch=(), out_kinds=None):
    spec = lambda kind: pl.BlockSpec(memory_space=SMEM if kind == "s" else VMEM)
    return pl.pallas_call(
        kernel,
        out_shape=outs,
        in_specs=[spec(k) for k in kinds],
        out_specs=jax.tree.map(lambda _: pl.BlockSpec(memory_space=VMEM), outs),
        scratch_shapes=list(scratch),
        compiler_params=pltpu.CompilerParams(vmem_limit_bytes=LIMIT),
    )(*args)


def shape(dims, dtype):
    return jax.ShapeDtypeStruct(dims, dtype)


def to_next(value, k):
    return lax.ppermute(value, "mp", [(i, (i + k) % N_MP) for i in range(N_MP)])


def to_other(value):
    size = lax.axis_size("dp")
    return lax.ppermute(value, "dp", [(i, i ^ 1) for i in range(size)])


def gathered(value):
    return [value] + [to_next(value, k) for k in range(1, N_MP)]


def gathered_halves(whole, half):
    got = [to_next(half, k) for k in range(1, N_MP)]
    out = [whole]
    for value in got:
        out += [value, to_other(value)]
    return out


def run_first(ids, plan, audio, gram, wp):
    return call(
        first_kernel,
        (
            shape((D, ROWS), bf16),
            shape((D, ROWS), bf16),
            shape((ROWS, D), bf16),
            shape((JOBS, D + ROWS, BLOCK), bf16),
        ),
        "ssss" + "v" * 12,
        (ids, *plan, *audio, gram, *wp),
        scratch=work_shapes(),
    )


def work_shapes():
    return [
        SMEM((JOBS,), jnp.int32),
        VMEM((4, WIN, 256), bf16),
        VMEM((D, BLOCK), bf16),
        VMEM((D, WIN), bf16),
        VMEM((MEL, BLOCK), f32),
        VMEM((MEL, 640), bf16),
        VMEM((D + ROWS, BLOCK), bf16),
    ]


def run_second(ids, plan, audio, gram, first, wa_t, wm, wo):
    return call(
        second_kernel,
        (shape((JOBS, 2 * MEL, 128), bf16),) + (shape((JOBS, PIECE, 128), bf16),) * 4,
        "ssss" + "v" * 18,
        (ids, *plan, *audio, gram, *first, wa_t, wm, *wo),
        scratch=work_shapes() + [VMEM((D + MEL, D + ROWS), bf16), VMEM((4 * PIECE, 128), bf16)],
    )


def shards(
    mel_audio, start_noise, span_start, span_length, block_route,
    w_input, attn_gain, w_qkv, w_out, final_gain, w_mel,
):
    e_rows = jnp.asarray(time_rows())
    ids = jnp.stack([lax.axis_index("dp"), lax.axis_index("mp")]).astype(jnp.int32)
    plan = (block_route, span_start, span_length)
    w3 = jnp.transpose(w_qkv, (1, 0, 2))
    whole, half = call(
        fold_kernel,
        (shape((3, ROWS, 256), bf16), shape((3, ROWS, 128), bf16)),
        "svvvv",
        (ids, w_input, e_rows, attn_gain.reshape(1, D), w3),
    )
    wp = gathered_halves(whole, half)
    audio = (mel_audio, to_other(mel_audio), start_noise, to_other(start_noise))
    wa_t, gram, wo_t, wo_half, wm = call(
        prep_kernel,
        (
            shape((D, ROWS), bf16),
            shape((2 * ROWS, ROWS), bf16),
            shape((D, 256), bf16),
            shape((D, 128), bf16),
            shape((MEL, D), bf16),
        ),
        "svvvvv",
        (ids, w_input, e_rows, w_out, w_mel, final_gain.reshape(1, D)),
    )
    wo = gathered_halves(wo_t, wo_half)
    slot_ids = ids[0] * WORK_DEV + jnp.arange(WORK_DEV, dtype=jnp.int32)
    matches = block_route[None, :] == slot_ids[:, None]
    every = jnp.arange(block_route.shape[0], dtype=jnp.int32)
    owners = jnp.sum(jnp.where(matches, every[None, :], 0), axis=1) // SLOT_DEV

    first = run_first(ids, plan, audio, gram, wp)
    tot, v0, v1, v2, v3 = run_second(ids, plan, audio, gram, first, wa_t, wm, wo)
    pieces = [v0] + [to_next(v, k) for k, v in ((1, v1), (2, v2), (3, v3))]
    pieces += [to_other(v) for v in pieces]
    totals = gathered(tot)
    totals += [to_other(t) for t in totals]
    packed = call(
        pack_kernel, shape((32, PIECE, 128), bf16), "ss" + "v" * 8, (ids, block_route, *pieces)
    )
    got = lax.all_to_all(packed, "dp", 0, 0, tiled=True)
    chosen = call(select_kernel, shape((WORK_DEV, PIECE, 128), bf16), "sv", (owners, got))
    parts = gathered(chosen)
    infilled = call(
        span_kernel,
        shape((UTT_DEV, MEL, SPAN_MAX), f32),
        "ss" + "v" * 8,
        (ids, block_route, *totals),
    )
    velocity = call(
        final_kernel,
        shape((WORK_DEV, MEL, BLOCK), f32),
        "svvvv",
        (ids, *parts),
        scratch=[VMEM((WORK_DEV, 4 * PIECE, 128), bf16)],
    )
    return (infilled, velocity)


def solution(mesh):
    return jax.shard_map(
        shards,
        mesh=mesh,
        in_specs=(
            P("dp", None, None),
            P("dp", None, None),
            P(),
            P(),
            P(),
            P(),
            P(),
            P(None, None, "mp"),
            P("mp", None),
            P(),
            P(),
        ),
        out_specs=(P("dp", None, None), P("dp", None, None)),
        check_vma=False,
    )
```

```python
import math

import jax
import jax.numpy as jnp
import numpy as np
from jax import lax
from jax.experimental import pallas as pl
from jax.experimental.pallas import tpu as pltpu
from jax.sharding import PartitionSpec as P

D = 1024
MEL = 80
HEAD_DIM = 64
HEADS = 16
BLOCK = 256
CTX = 128
BLK_UTT = 4
UTT_DEV = 4
WORK_DEV = 6
EULER = 2
FRAMES = 2048
WIN = 512
SPAN_MAX = 1024
SLOT_DEV = 16
N_MP = 4
JOBS = 4
ROWS = 176
PIECE = 48
flow_steps = 32.0
norm_eps = 1e-05
f32 = jnp.float32
bf16 = jnp.bfloat16
VMEM = pltpu.VMEM
SMEM = pltpu.SMEM
MAIN_LIMIT = 44
SLOT_AT, JOB_AT, COUNT_AT, OWNER_AT, TABLE = 32, 64, 68, 72, 80


def time_rows():
    half = D // 2
    freqs = np.exp(-math.log(10000.0) * np.arange(half, dtype=np.float32) / half)
    rows = np.zeros((16, D), np.float32)
    for step in range(EULER):
        angles = np.float32(1000.0 * step / flow_steps) * freqs.astype(np.float32)
        e = np.concatenate([np.sin(angles), np.cos(angles)])
        e = e - e.mean()
        rows[2 * step] = e
        rows[2 * step + 1] = e
    return rows


def high_low(rows):
    high = rows.astype(bf16).astype(f32)
    odd = lax.broadcasted_iota(jnp.int32, rows.shape, 0) % 2 == 1
    return jnp.where(odd, rows - high, high)


def fold_kernel(w_in, e_rows, gain, w_qkv, out, half):
    core = lax.axis_index("dp") & 1
    w = w_in[...].astype(f32)
    wc = w - jnp.mean(w, axis=1, keepdims=True)
    g = gain[...]
    wag = jnp.concatenate([wc * g, high_low(e_rows[...] * g)], axis=0).astype(bf16)
    for c in range(3):
        res = jnp.dot(wag, w_qkv[c], preferred_element_type=f32)
        if c == 0:
            res = res * (math.log2(math.e) / math.sqrt(HEAD_DIM))
        e_res = res[160:176]
        row = lax.broadcasted_iota(jnp.int32, e_res.shape, 0)
        first = e_res[0:1] + e_res[1:2]
        second = e_res[2:3] + e_res[3:4]
        both = jnp.where(row < 2, first, jnp.where(row < 4, second, 0.0))
        out[c, 0:160, :] = res[0:160].astype(bf16)
        out[c, 160:176, :] = high_low(both).astype(bf16)
        half[c] = jnp.where(core == 0, out[c, :, 0:128], out[c, :, 128:256])


def prep_kernel(w_in, e_rows, w_out, w_mel, gain, wa_t, gram, wo_t, half, wm):
    w = w_in[...].astype(f32)
    wc = w - jnp.mean(w, axis=1, keepdims=True)
    wa = jnp.concatenate([wc, high_low(e_rows[...]), jnp.zeros((80, D), f32)], axis=0)
    wa_t[...] = wa.T[:, :ROWS].astype(bf16)
    wab = wa.astype(bf16)
    g = lax.dot_general(wab, wab, (((1,), (1,)), ((), ())), preferred_element_type=f32)
    g = g[0:ROWS, 0:ROWS] * (1.0 / D)
    high = g.astype(bf16)
    gram[0:ROWS, :] = high
    gram[ROWS : 2 * ROWS, :] = (g - high.astype(f32)).astype(bf16)
    core = lax.axis_index("dp") & 1
    o = w_out[...].astype(f32)
    o = o - jnp.mean(o, axis=1, keepdims=True)
    wo_t[...] = o.T.astype(bf16)
    half[...] = jnp.where(core == 0, wo_t[:, 0:128], wo_t[:, 128:256])
    wm[...] = (w_mel[...].astype(f32) * gain[...]).astype(bf16)


def plan_kernel(
    route, starts, lengths, mel_a, mel_b, noise_a, noise_b, gram,
    table, context_out, noise_out, valid_out, scaled_out, values_out, keys_out, own_out,
    chunk_s, x_s,
):
    dp = lax.axis_index("dp")
    m = lax.axis_index("mp")
    core = dp & 1
    base = (dp >> 1) * (2 * SLOT_DEV)
    seat = core * N_MP + m
    for i in range(TABLE):
        table[i] = -1

    def scan(s, rank):
        dest = route[base + s]
        live = dest >= 0
        q = rank >> 3

        @pl.when(jnp.logical_and(live, (rank & 7) == seat))
        def _():
            table[JOB_AT + q] = s

        @pl.when(jnp.logical_and(live, (s >> 4) == core))
        def _():
            away = ((rank >> 2) & 1) ^ core
            entry = (away * 4 + ((m - rank) & 3)) * JOBS + q
            table[entry] = (dest * 10923) >> 16
            table[SLOT_AT + entry] = s & 15

        return rank + live.astype(jnp.int32)

    n_live = lax.fori_loop(0, 2 * SLOT_DEV, scan, jnp.int32(0))
    n_jobs = (n_live - seat + 7) >> 3
    table[COUNT_AT] = n_jobs

    def owner(g, carry):
        j = route[g] - dp * WORK_DEV

        @pl.when(jnp.logical_and(j >= 0, j < WORK_DEV))
        def _():
            table[OWNER_AT + j] = g >> 4

        return carry

    lax.fori_loop(0, 32 * SLOT_DEV, owner, 0)

    def job(q, carry):
        s = table[JOB_AT + q]
        u = (s >> 2) & 3
        order = s & 3
        utter = (dp >> 1) * (2 * UTT_DEV) + (s >> 2)
        span = starts[utter]
        length = lengths[utter]
        first = span + BLOCK * order - CTX
        aligned = pl.multiple_of(jnp.clip((first >> 7) << 7, 0, FRAMES - 640), 128)
        off = pl.multiple_of(order * BLOCK, BLOCK)
        here = (s >> 4) == core

        @pl.when(here)
        def _():
            chunk_s[...] = mel_a[u, :, pl.ds(aligned, 640)]
            x_s[...] = noise_a[u, :, pl.ds(off, BLOCK)]

        @pl.when(jnp.logical_not(here))
        def _():
            chunk_s[...] = mel_b[u, :, pl.ds(aligned, 640)]
            x_s[...] = noise_b[u, :, pl.ds(off, BLOCK)]

        own = lax.broadcasted_iota(jnp.int32, (1, BLOCK), 1) < length - BLOCK * order
        x = jnp.where(own, x_s[...].astype(f32), 0.0)
        noise_out[q] = x.astype(bf16)
        shift = aligned - first
        shift = jnp.where(shift < 0, shift + 640, shift)
        chunk = pltpu.roll(chunk_s[...].astype(f32), shift, 1)[:, :WIN]
        pos = first + lax.broadcasted_iota(jnp.int32, (1, WIN), 1)
        valid = jnp.logical_and(pos >= 0, pos < FRAMES)
        in_span = jnp.logical_and(pos >= span, pos < span + length)
        keep = jnp.logical_and(valid, jnp.logical_not(in_span))
        context = jnp.where(keep, chunk, 0.0)
        context_out[q] = context.astype(bf16)
        valid = valid.astype(f32)
        in_block = jnp.logical_and(pos >= first + CTX, jnp.logical_and(pos < first + CTX + BLOCK, in_span))
        row = lax.broadcasted_iota(jnp.int32, (8, WIN), 0)
        valid_out[q] = jnp.where(row == 0, valid, in_block.astype(f32))
        window(0, context, valid, x, gram, scaled_out.at[q], values_out.at[q], keys_out.at[q], own_out.at[q])
        return carry

    lax.fori_loop(0, n_jobs, job, 0)


def window(n, context, valid, x, gram, scaled_out, values_out, keys_out, own_out):
    side = jnp.zeros((MEL, CTX), f32)
    state = jnp.concatenate([side, x.astype(bf16).astype(f32), side], axis=1)
    flags = (lax.broadcasted_iota(jnp.int32, (16, WIN), 0) >> 1) == n
    win = jnp.concatenate([context, state, flags.astype(f32)], axis=0)
    win = jnp.where(valid > 0.0, win, win[:, CTX : CTX + 1])
    win_b = win.astype(bf16)
    own_out[...] = win_b[:, CTX : CTX + BLOCK]
    gw = jnp.dot(gram[...], win_b, preferred_element_type=f32)
    var = jnp.sum(win * (gw[0:ROWS] + gw[ROWS : 2 * ROWS]), axis=0, keepdims=True)
    scaled = win * lax.rsqrt(jnp.maximum(var, 0.0) + norm_eps)
    scaled_out[...] = scaled[:, CTX : CTX + BLOCK].astype(bf16)
    values_out[...] = (scaled * valid).astype(bf16)
    padded = jnp.concatenate([scaled, jnp.zeros((256 - ROWS, WIN), f32)], axis=0)
    keys_out[...] = padded.T.astype(bf16)[:, :ROWS]


def attend(scaled, values, win_t, valid, weights, work, o_out):
    wq_s, wv_s, wk_s = weights
    k_s, q_s, v_s = work
    q_s[...] = jnp.dot(wq_s[...], scaled[...], preferred_element_type=f32).astype(bf16)
    keys = jnp.dot(win_t[...], wk_s[...], preferred_element_type=f32).astype(bf16)
    for p in range(4):
        k_s[p] = keys[:, 256 * p : 256 * p + 256]
    v_s[...] = jnp.dot(wv_s[...], values[...], preferred_element_type=f32).astype(bf16)
    ones_rows = jnp.broadcast_to(valid, (16, WIN)).astype(bf16)
    zero = jnp.zeros((HEAD_DIM, BLOCK), bf16)
    for g in range(4):
        columns = []
        for j in range(4):
            at = 256 * g + 64 * j
            rows = [q_s[at : at + 64, :] if t == j else zero for t in range(4)]
            columns.append(jnp.concatenate(rows, axis=0))
        sc = jnp.dot(k_s[g], jnp.concatenate(columns, axis=1), preferred_element_type=f32)
        top = jnp.max(sc, axis=0, keepdims=True)
        pr = jnp.exp2(sc - top).astype(bf16)
        for j in range(4):
            at = 256 * g + 64 * j
            lhs = jnp.concatenate([v_s[at : at + 64, :], ones_rows], axis=0)
            ov = jnp.dot(lhs, pr[:, 256 * j : 256 * j + 256], preferred_element_type=f32)
            o_out[at : at + 64, :] = (ov[0:64] / ov[64:65]).astype(bf16)


def velocity_of(wr_s, o, own):
    r = jnp.dot(wr_s[...], o[...], preferred_element_type=f32)
    body = r[0:D]
    var = jnp.sum(body * body, axis=0, keepdims=True) * (1.0 / D)
    return jnp.where(own, r[D : D + MEL] * lax.rsqrt(var + norm_eps), 0.0)


def first_kernel(
    table, valid, scaled, values, keys, own_win,
    wp0, hp1, sp1, hp2, sp2, hp3, sp3,
    wq_s, wv_s, wk_s, o_out,
    k_s, q_s, v_s,
):
    at = 0
    for wp in (wp0, hp1, sp1, hp2, sp2, hp3, sp3):
        width = wp.shape[2]
        lanes = slice(at, at + width)
        pad = jnp.zeros((256 - ROWS, width), f32)
        wq_s[lanes, :] = jnp.concatenate([wp[0].astype(f32), pad], axis=0).T.astype(bf16)[:, :ROWS]
        wv_s[lanes, :] = jnp.concatenate([wp[2].astype(f32), pad], axis=0).T.astype(bf16)[:, :ROWS]
        wk_s[:, lanes] = wp[1]
        at += width

    def job(q, carry):
        o = o_out.at[q]
        o[1024 : 1024 + ROWS, :] = own_win[q]
        attend(
            scaled.at[q], values.at[q], keys.at[q], valid[q, 0:1, :],
            (wq_s, wv_s, wk_s), (k_s, q_s, v_s), o,
        )
        return carry

    lax.fori_loop(0, table[COUNT_AT], job, 0)


def second_kernel(
    table, context, noise, valid, gram, wq_s, wv_s, wk_s, o_in, wa_t, wm,
    wo0, ho1, so1, ho2, so2, ho3, so3,
    tot_out, v0, v1, v2, v3,
    k_s, q_s, v_s, o_s, wr_s, stage, scaled_s, values_s, keys_s,
):
    m = lax.axis_index("mp")
    at = 0
    for wo in (wo0, ho1, so1, ho2, so2, ho3, so3):
        width = wo.shape[1]
        wr_s[0:D, at : at + width] = wo[...]
        at += width
    wr_s[0:D, 1024 : 1024 + ROWS] = wa_t[...]
    wr_s[D : D + MEL, :] = jnp.dot(wm[...], wr_s[0:D, :], preferred_element_type=f32).astype(bf16)
    stage[...] = jnp.zeros(stage.shape, bf16)

    def job(q, carry):
        masks = valid[q]
        own = masks[1:2, CTX : CTX + BLOCK] > 0.0
        usable = masks[0:1, :]
        first = velocity_of(wr_s, o_in.at[q], own)
        x = noise[q].astype(f32) + first * (1.0 / flow_steps)
        window(
            1, context[q].astype(f32), usable, x, gram,
            scaled_s, values_s, keys_s, o_s.at[1024 : 1024 + ROWS, :],
        )
        attend(
            scaled_s, values_s, keys_s, usable, (wq_s, wv_s, wk_s), (k_s, q_s, v_s), o_s
        )
        last = velocity_of(wr_s, o_s, own)
        total = (first + last).astype(bf16)
        tot_out[q, 0:MEL, :] = total[:, 0:128]
        tot_out[q, MEL : 2 * MEL, :] = total[:, 128:256]
        vel = last.astype(bf16)
        stage[0:MEL, :] = vel[:, 0:128]
        stage[MEL : 2 * MEL, :] = vel[:, 128:256]
        for k, out in enumerate((v0, v1, v2, v3)):
            quarter = (m + k) & 3
            out[q] = stage[pl.ds(pl.multiple_of(quarter * PIECE, 16), PIECE), :]
        return carry

    lax.fori_loop(0, table[COUNT_AT], job, 0)


def pack_kernel(table, a0, a1, a2, a3, b0, b1, b2, b3, out, sems):
    def each(act):
        for i, a in enumerate((a0, a1, a2, a3, b0, b1, b2, b3)):
            for q in range(JOBS):
                entry = i * JOBS + q
                worker = table[entry]

                @pl.when(worker >= 0)
                def _():
                    act(pltpu.make_async_copy(a.at[q], out.at[worker], sems.at[entry]))

    each(lambda copy: copy.start())
    each(lambda copy: copy.wait())


def select_kernel(table, got, out, sems):
    copies = [
        pltpu.make_async_copy(got.at[table[OWNER_AT + j]], out.at[j], sems.at[j])
        for j in range(WORK_DEV)
    ]
    for copy in copies:
        copy.start()
    for copy in copies:
        copy.wait()


def span_kernel(table, a0, a1, a2, a3, b0, b1, b2, b3, out):
    out[...] = jnp.zeros(out.shape, f32)
    for i, a in enumerate((a0, a1, a2, a3, b0, b1, b2, b3)):
        for q in range(JOBS):
            s = table[SLOT_AT + i * JOBS + q]

            @pl.when(s >= 0)
            def _():
                block = a[q].astype(f32)
                off = (s & 3) * BLOCK
                out[s >> 2, :, pl.ds(pl.multiple_of(off, 128), 128)] = block[0:MEL]
                out[s >> 2, :, pl.ds(pl.multiple_of(off + 128, 128), 128)] = block[MEL : 2 * MEL]


def final_kernel(b0, b1, b2, b3, out, stage):
    m = lax.axis_index("mp")
    for k, b in enumerate((b0, b1, b2, b3)):
        quarter = (m - k) & 3
        at = pl.multiple_of(quarter * PIECE, 16)
        for j in range(WORK_DEV):
            stage[j, pl.ds(at, PIECE), :] = b[j]
    for j in range(WORK_DEV):
        out[j, :, 0:128] = stage[j, 0:MEL, :].astype(f32)
        out[j, :, 128:256] = stage[j, MEL : 2 * MEL, :].astype(f32)


def call(kernel, outs, kinds, args, scratch=(), out_kinds=None, limit=24):
    spaces = {"s": SMEM, "v": VMEM, "h": pl.ANY}
    spec = lambda kind: pl.BlockSpec(memory_space=spaces[kind])
    many = isinstance(outs, tuple)
    out_kinds = out_kinds or "v" * (len(outs) if many else 1)
    out_specs = tuple(spec(k) for k in out_kinds)
    return pl.pallas_call(
        kernel,
        out_shape=outs,
        in_specs=[spec(k) for k in kinds],
        out_specs=out_specs if many else out_specs[0],
        scratch_shapes=list(scratch),
        compiler_params=pltpu.CompilerParams(vmem_limit_bytes=limit * 1024 * 1024),
    )(*args)


def shape(dims, dtype):
    return jax.ShapeDtypeStruct(dims, dtype)


def to_next(value, k):
    return lax.ppermute(value, "mp", [(i, (i + k) % N_MP) for i in range(N_MP)])


def to_other(value):
    size = lax.axis_size("dp")
    return lax.ppermute(value, "dp", [(i, i ^ 1) for i in range(size)])


def gathered(value):
    return [value] + [to_next(value, k) for k in range(1, N_MP)]


def after(value, *others):
    return lax.optimization_barrier((value, *others))[0]


def run_plan(plan, audio, gram):
    return call(
        plan_kernel,
        (
            shape((TABLE,), jnp.int32),
            shape((JOBS, MEL, WIN), bf16),
            shape((JOBS, MEL, BLOCK), bf16),
            shape((JOBS, 8, WIN), f32),
            shape((JOBS, ROWS, BLOCK), bf16),
            shape((JOBS, ROWS, WIN), bf16),
            shape((JOBS, WIN, ROWS), bf16),
            shape((JOBS, ROWS, BLOCK), bf16),
        ),
        "sss" + "v" * 5,
        (*plan, *audio, gram),
        scratch=[VMEM((MEL, 640), bf16), VMEM((MEL, BLOCK), bf16)],
        out_kinds="s" + "v" * 7,
    )


def run_first(table, windows, wp):
    return call(
        first_kernel,
        (
            shape((D, ROWS), bf16),
            shape((D, ROWS), bf16),
            shape((ROWS, D), bf16),
            shape((JOBS, D + ROWS, BLOCK), bf16),
        ),
        "s" + "v" * 12,
        (table, *windows, *wp),
        scratch=work_shapes(),
        limit=MAIN_LIMIT,
    )


def work_shapes():
    return [VMEM((4, WIN, 256), bf16), VMEM((D, BLOCK), bf16), VMEM((D, WIN), bf16)]


def run_second(table, context, noise, valid, gram, first, wa_t, wm, wo):
    return call(
        second_kernel,
        (shape((JOBS, 2 * MEL, 128), bf16),) + (shape((JOBS, PIECE, 128), bf16),) * 4,
        "s" + "v" * 17,
        (table, context, noise, valid, gram, *first, wa_t, wm, *wo),
        scratch=work_shapes()
        + [
            VMEM((D + ROWS, BLOCK), bf16),
            VMEM((D + MEL, D + ROWS), bf16),
            VMEM((4 * PIECE, 128), bf16),
            VMEM((ROWS, BLOCK), bf16),
            VMEM((ROWS, WIN), bf16),
            VMEM((WIN, ROWS), bf16),
        ],
        limit=MAIN_LIMIT,
    )


def shards(
    mel_audio, start_noise, span_start, span_length, block_route,
    w_input, attn_gain, w_qkv, w_out, final_gain, w_mel,
):
    e_rows = jnp.asarray(time_rows())
    plan = (block_route, span_start, span_length)
    w3 = jnp.transpose(w_qkv, (1, 0, 2))
    whole, half = call(
        fold_kernel,
        (shape((3, ROWS, 256), bf16), shape((3, ROWS, 128), bf16)),
        "vvvv",
        (w_input, e_rows, attn_gain.reshape(1, D), w3),
    )
    halves = gathered(half)[1:]
    audio = (mel_audio, to_other(mel_audio), start_noise, to_other(start_noise))
    wa_t, gram, wo_t, wo_half, wm = call(
        prep_kernel,
        (
            shape((D, ROWS), bf16),
            shape((2 * ROWS, ROWS), bf16),
            shape((D, 256), bf16),
            shape((D, 128), bf16),
            shape((MEL, D), bf16),
        ),
        "vvvvv",
        (w_input, e_rows, after(w_out, half), w_mel, final_gain.reshape(1, D)),
    )
    out_halves = gathered(wo_half)[1:]
    table, context, noise, valid, scaled, values, keys, own_win = run_plan(plan, audio, gram)
    wp = [whole]
    for h in halves:
        wp += [h, to_other(h)]
    first = run_first(table, (valid, scaled, values, keys, own_win), wp)
    out_halves = lax.optimization_barrier((*out_halves, first[3]))
    first = (*first[:3], out_halves[-1])
    wo = [wo_t]
    for h in out_halves[:-1]:
        wo += [h, to_other(h)]
    tot, v0, v1, v2, v3 = run_second(table, context, noise, valid, gram, first, wa_t, wm, wo)
    pieces = [v0] + [to_next(v, k) for k, v in ((1, v1), (2, v2), (3, v3))]
    pieces += [to_other(v) for v in pieces]
    packed = call(
        pack_kernel,
        shape((32, PIECE, 128), bf16),
        "s" + "h" * 8,
        (table, *pieces),
        scratch=[pltpu.SemaphoreType.DMA((8 * JOBS,))],
        out_kinds="h",
    )
    got = lax.all_to_all(packed, "dp", 0, 0, tiled=True)
    totals = gathered(after(tot, packed))
    totals += [to_other(t) for t in totals]
    infilled = call(
        span_kernel, shape((UTT_DEV, MEL, SPAN_MAX), f32), "s" + "v" * 8, (table, *totals)
    )
    chosen = call(
        select_kernel,
        shape((WORK_DEV, PIECE, 128), bf16),
        "sh",
        (table, got),
        scratch=[pltpu.SemaphoreType.DMA((WORK_DEV,))],
        out_kinds="h",
    )
    parts = gathered(chosen)
    velocity = call(
        final_kernel,
        shape((WORK_DEV, MEL, BLOCK), f32),
        "vvvv",
        tuple(parts),
        scratch=[VMEM((WORK_DEV, 4 * PIECE, 128), bf16)],
    )
    return (infilled, velocity)


def solution(mesh):
    return jax.shard_map(
        shards,
        mesh=mesh,
        in_specs=(
            P("dp", None, None),
            P("dp", None, None),
            P(),
            P(),
            P(),
            P(),
            P(),
            P(None, None, "mp"),
            P("mp", None),
            P(),
            P(),
        ),
        out_specs=(P("dp", None, None), P("dp", None, None)),
        check_vma=False,
    )
```

```python
import math

import jax
import jax.numpy as jnp
import numpy as np
from jax import lax
from jax.experimental import pallas as pl
from jax.experimental.pallas import tpu as pltpu
from jax.sharding import PartitionSpec as P

D = 1024
MEL = 80
HEAD_DIM = 64
HEADS = 16
BLOCK = 256
CTX = 128
BLK_UTT = 4
UTT_DEV = 4
WORK_DEV = 6
EULER = 2
FRAMES = 2048
WIN = 512
SPAN_MAX = 1024
SLOT_DEV = 16
N_MP = 4
JOBS = 4
ROWS = 176
PIECE = 48
SENT = PIECE + 2 * MEL
flow_steps = 32.0
norm_eps = 1e-05
f32 = jnp.float32
bf16 = jnp.bfloat16
VMEM = pltpu.VMEM
SMEM = pltpu.SMEM
MAIN_LIMIT = 44
SLOT_AT, JOB_AT, COUNT_AT, OWNER_AT, TABLE = 32, 64, 68, 72, 80


def time_rows():
    half = D // 2
    freqs = np.exp(-math.log(10000.0) * np.arange(half, dtype=np.float32) / half)
    rows = np.zeros((16, D), np.float32)
    for step in range(EULER):
        angles = np.float32(1000.0 * step / flow_steps) * freqs.astype(np.float32)
        e = np.concatenate([np.sin(angles), np.cos(angles)])
        e = e - e.mean()
        rows[2 * step] = e
        rows[2 * step + 1] = e
    return rows


def high_low(rows):
    high = rows.astype(bf16).astype(f32)
    odd = lax.broadcasted_iota(jnp.int32, rows.shape, 0) % 2 == 1
    return jnp.where(odd, rows - high, high)


def fold_kernel(w_in_h, e_rows_h, gain_h, w_qkv_h, out, half, w_in, e_rows, gain, w_qkv, sems):
    pairs = [(w_in_h, w_in), (e_rows_h, e_rows), (gain_h, gain)]
    pairs += [(w_qkv_h.at[c], w_qkv.at[c]) for c in range(3)]
    copies = [pltpu.make_async_copy(a, b, sems.at[i]) for i, (a, b) in enumerate(pairs)]
    for copy in copies:
        copy.start()
    for copy in copies[0:3]:
        copy.wait()
    core = lax.axis_index("dp") & 1
    w = w_in[...].astype(f32)
    wc = w - jnp.mean(w, axis=1, keepdims=True)
    g = gain[...]
    wag = jnp.concatenate([wc * g, high_low(e_rows[...] * g)], axis=0).astype(bf16)
    for c in range(3):
        copies[3 + c].wait()
        res = jnp.dot(wag, w_qkv[c], preferred_element_type=f32)
        if c == 0:
            res = res * (math.log2(math.e) / math.sqrt(HEAD_DIM))
        e_res = res[160:176]
        row = lax.broadcasted_iota(jnp.int32, e_res.shape, 0)
        first = e_res[0:1] + e_res[1:2]
        second = e_res[2:3] + e_res[3:4]
        both = jnp.where(row < 2, first, jnp.where(row < 4, second, 0.0))
        out[c, 0:160, :] = res[0:160].astype(bf16)
        out[c, 160:176, :] = high_low(both).astype(bf16)
        half[c] = jnp.where(core == 0, out[c, :, 0:128], out[c, :, 128:256])


def prep_kernel(w_in, e_rows, w_out, w_mel, gain, wa_t, wo_t, half, wm):
    w = w_in[...].astype(f32)
    wc = w - jnp.mean(w, axis=1, keepdims=True)
    wa = jnp.concatenate([wc, high_low(e_rows[...]), jnp.zeros((80, D), f32)], axis=0)
    wa_t[...] = wa.T[:, :ROWS].astype(bf16)
    core = lax.axis_index("dp") & 1
    o = w_out[...].astype(f32)
    o = o - jnp.mean(o, axis=1, keepdims=True)
    wo_t[...] = o.T.astype(bf16)
    half[...] = jnp.where(core == 0, wo_t[:, 0:128], wo_t[:, 128:256])
    wm[...] = (w_mel[...].astype(f32) * gain[...]).astype(bf16)


def plan_kernel(
    route, starts, lengths, mel_a, mel_b, noise_a, noise_b, w_in, e_rows, route_v,
    table, gram, context_out, noise_out, valid_out, scaled_out, values_out, keys_out, own_out,
    chunk_s, x_s,
):
    dp = lax.axis_index("dp")
    m = lax.axis_index("mp")
    core = dp & 1
    w = w_in[...].astype(f32)
    wc = w - jnp.mean(w, axis=1, keepdims=True)
    wa = jnp.concatenate([wc, high_low(e_rows[...]), jnp.zeros((80, D), f32)], axis=0)
    wab = wa.astype(bf16)
    g = lax.dot_general(wab, wab, (((1,), (1,)), ((), ())), preferred_element_type=f32)
    g = g[0:ROWS, 0:ROWS] * (1.0 / D)
    high = g.astype(bf16)
    gram[0:ROWS, :] = high
    gram[ROWS : 2 * ROWS, :] = (g - high.astype(f32)).astype(bf16)
    base = (dp >> 1) * (2 * SLOT_DEV)
    seat = core * N_MP + m
    for i in range(TABLE):
        table[i] = -1

    def scan(s, rank):
        dest = route[base + s]
        live = dest >= 0
        q = rank >> 3

        @pl.when(jnp.logical_and(live, (rank & 7) == seat))
        def _():
            table[JOB_AT + q] = s

        @pl.when(jnp.logical_and(live, (s >> 4) == core))
        def _():
            away = ((rank >> 2) & 1) ^ core
            entry = (away * 4 + ((m - rank) & 3)) * JOBS + q
            table[entry] = (dest * 10923) >> 16
            table[SLOT_AT + entry] = s & 15

        return rank + live.astype(jnp.int32)

    n_live = lax.fori_loop(0, 2 * SLOT_DEV, scan, jnp.int32(0))
    n_jobs = (n_live - seat + 7) >> 3
    table[COUNT_AT] = n_jobs

    places = route_v[...]
    owner = (
        lax.broadcasted_iota(jnp.int32, places.shape, 0) * places.shape[1]
        + lax.broadcasted_iota(jnp.int32, places.shape, 1)
    ) >> 4
    for j in range(WORK_DEV):
        found = jnp.where(places == dp * WORK_DEV + j, owner, 0)
        table[OWNER_AT + j] = jnp.sum(found)

    def job(q, carry):
        s = table[JOB_AT + q]
        u = (s >> 2) & 3
        order = s & 3
        utter = (dp >> 1) * (2 * UTT_DEV) + (s >> 2)
        span = starts[utter]
        length = lengths[utter]
        first = span + BLOCK * order - CTX
        aligned = pl.multiple_of(jnp.clip((first >> 7) << 7, 0, FRAMES - 640), 128)
        off = pl.multiple_of(order * BLOCK, BLOCK)
        here = (s >> 4) == core

        @pl.when(here)
        def _():
            chunk_s[...] = mel_a[u, :, pl.ds(aligned, 640)]
            x_s[...] = noise_a[u, :, pl.ds(off, BLOCK)]

        @pl.when(jnp.logical_not(here))
        def _():
            chunk_s[...] = mel_b[u, :, pl.ds(aligned, 640)]
            x_s[...] = noise_b[u, :, pl.ds(off, BLOCK)]

        own = lax.broadcasted_iota(jnp.int32, (1, BLOCK), 1) < length - BLOCK * order
        x = jnp.where(own, x_s[...].astype(f32), 0.0)
        noise_out[q] = x.astype(bf16)
        shift = aligned - first
        shift = jnp.where(shift < 0, shift + 640, shift)
        chunk = pltpu.roll(chunk_s[...].astype(f32), shift, 1)[:, :WIN]
        pos = first + lax.broadcasted_iota(jnp.int32, (1, WIN), 1)
        valid = jnp.logical_and(pos >= 0, pos < FRAMES)
        in_span = jnp.logical_and(pos >= span, pos < span + length)
        keep = jnp.logical_and(valid, jnp.logical_not(in_span))
        context = jnp.where(keep, chunk, 0.0)
        context_out[q] = context.astype(bf16)
        valid = valid.astype(f32)
        in_block = jnp.logical_and(pos >= first + CTX, jnp.logical_and(pos < first + CTX + BLOCK, in_span))
        row = lax.broadcasted_iota(jnp.int32, (8, WIN), 0)
        valid_out[q] = jnp.where(row == 0, valid, in_block.astype(f32))
        window(0, context, valid, x, gram, scaled_out.at[q], values_out.at[q], keys_out.at[q], own_out.at[q])
        return carry

    lax.fori_loop(0, n_jobs, job, 0)


def window(n, context, valid, x, gram, scaled_out, values_out, keys_out, own_out):
    side = jnp.zeros((MEL, CTX), f32)
    state = jnp.concatenate([side, x.astype(bf16).astype(f32), side], axis=1)
    flags = (lax.broadcasted_iota(jnp.int32, (16, WIN), 0) >> 1) == n
    win = jnp.concatenate([context, state, flags.astype(f32)], axis=0)
    win = jnp.where(valid > 0.0, win, win[:, CTX : CTX + 1])
    win_b = win.astype(bf16)
    own_out[...] = win_b[:, CTX : CTX + BLOCK]
    gw = jnp.dot(gram[...], win_b, preferred_element_type=f32)
    var = jnp.sum(win * (gw[0:ROWS] + gw[ROWS : 2 * ROWS]), axis=0, keepdims=True)
    scaled = win * lax.rsqrt(jnp.maximum(var, 0.0) + norm_eps)
    scaled_out[...] = scaled[:, CTX : CTX + BLOCK].astype(bf16)
    values_out[...] = (scaled * valid).astype(bf16)
    padded = jnp.concatenate([scaled, jnp.zeros((256 - ROWS, WIN), f32)], axis=0)
    keys_out[...] = padded.T.astype(bf16)[:, :ROWS]


def attend(scaled, values, win_t, valid, weights, work, o_out):
    wq_s, wv_s, wk_s = weights
    k_s, q_s, v_s = work
    q_s[...] = jnp.dot(wq_s[...], scaled[...], preferred_element_type=f32).astype(bf16)
    keys = jnp.dot(win_t[...], wk_s[...], preferred_element_type=f32).astype(bf16)
    for p in range(4):
        k_s[p] = keys[:, 256 * p : 256 * p + 256]
    v_s[...] = jnp.dot(wv_s[...], values[...], preferred_element_type=f32).astype(bf16)
    ones_rows = jnp.broadcast_to(valid, (16, WIN)).astype(bf16)
    zero = jnp.zeros((HEAD_DIM, BLOCK), bf16)

    def score(g):
        columns = []
        for j in range(4):
            at = 256 * g + 64 * j
            rows = [q_s[at : at + 64, :] if t == j else zero for t in range(4)]
            columns.append(jnp.concatenate(rows, axis=0))
        return jnp.dot(k_s[g], jnp.concatenate(columns, axis=1), preferred_element_type=f32)

    ahead = score(0)
    for g in range(4):
        sc = ahead
        if g < 3:
            ahead = score(g + 1)
        top = jnp.max(sc, axis=0, keepdims=True)
        pr = jnp.exp2(sc - top).astype(bf16)
        for j in range(4):
            at = 256 * g + 64 * j
            lhs = jnp.concatenate([v_s[at : at + 64, :], ones_rows], axis=0)
            ov = jnp.dot(lhs, pr[:, 256 * j : 256 * j + 256], preferred_element_type=f32)
            o_out[at : at + 64, :] = (ov[0:64] / ov[64:65]).astype(bf16)


def velocity_of(wr_s, o, own):
    v = jnp.dot(wr_s[D : D + MEL, :], o[...], preferred_element_type=f32)
    squares = jnp.zeros((8, BLOCK), f32)
    part = D // 4
    for i in range(4):
        r = jnp.dot(wr_s[part * i : part * i + part, :], o[...], preferred_element_type=f32)
        squares = squares + jnp.sum((r * r).reshape(part // 8, 8, BLOCK), axis=0)
    var = jnp.sum(squares, axis=0, keepdims=True) * (1.0 / D)
    return jnp.where(own, v * lax.rsqrt(var + norm_eps), 0.0)


def first_kernel(
    table, valid, scaled, values, keys, own_win,
    wp0, hp1, sp1, hp2, sp2, hp3, sp3,
    wq_s, wv_s, wk_s, o_out,
    k_s, q_s, v_s,
):
    at = 0
    for wp in (wp0, hp1, sp1, hp2, sp2, hp3, sp3):
        width = wp.shape[2]
        lanes = slice(at, at + width)
        pad = jnp.zeros((256 - ROWS, width), f32)
        wq_s[lanes, :] = jnp.concatenate([wp[0].astype(f32), pad], axis=0).T.astype(bf16)[:, :ROWS]
        wv_s[lanes, :] = jnp.concatenate([wp[2].astype(f32), pad], axis=0).T.astype(bf16)[:, :ROWS]
        wk_s[:, lanes] = wp[1]
        at += width

    def job(q, carry):
        o = o_out.at[q]
        o[1024 : 1024 + ROWS, :] = own_win[q]
        attend(
            scaled.at[q], values.at[q], keys.at[q], valid[q, 0:1, :],
            (wq_s, wv_s, wk_s), (k_s, q_s, v_s), o,
        )
        return carry

    lax.fori_loop(0, table[COUNT_AT], job, 0)


def second_kernel(
    table, context, noise, valid, gram, wq_s, wv_s, wk_s, o_in, wa_t, wm,
    wo0, ho1, so1, ho2, so2, ho3, so3,
    v0, v1, v2, v3,
    k_s, q_s, v_s, o_s, wr_s, stage, scaled_s, values_s, keys_s,
):
    m = lax.axis_index("mp")
    at = 0
    for wo in (wo0, ho1, so1, ho2, so2, ho3, so3):
        width = wo.shape[1]
        wr_s[0:D, at : at + width] = wo[...]
        at += width
    wr_s[0:D, 1024 : 1024 + ROWS] = wa_t[...]
    wr_s[D : D + MEL, :] = jnp.dot(wm[...], wr_s[0:D, :], preferred_element_type=f32).astype(bf16)
    stage[...] = jnp.zeros(stage.shape, bf16)

    def job(q, carry):
        masks = valid[q]
        own = masks[1:2, CTX : CTX + BLOCK] > 0.0
        usable = masks[0:1, :]
        first = velocity_of(wr_s, o_in.at[q], own)
        x = noise[q].astype(f32) + first * (1.0 / flow_steps)
        window(
            1, context[q].astype(f32), usable, x, gram,
            scaled_s, values_s, keys_s, o_s.at[1024 : 1024 + ROWS, :],
        )
        attend(
            scaled_s, values_s, keys_s, usable, (wq_s, wv_s, wk_s), (k_s, q_s, v_s), o_s
        )
        last = velocity_of(wr_s, o_s, own)
        total = (first + last).astype(bf16)
        vel = last.astype(bf16)
        stage[0:MEL, :] = vel[:, 0:128]
        stage[MEL : 2 * MEL, :] = vel[:, 128:256]
        for k, out in enumerate((v0, v1, v2, v3)):
            quarter = (m + k) & 3
            out[q, 0:PIECE, :] = stage[pl.ds(pl.multiple_of(quarter * PIECE, 16), PIECE), :]
            out[q, PIECE : PIECE + MEL, :] = total[:, 0:128]
            out[q, PIECE + MEL : SENT, :] = total[:, 128:256]
        return carry

    lax.fori_loop(0, table[COUNT_AT], job, 0)


def pack_kernel(table, a0, a1, a2, a3, b0, b1, b2, b3, out, sems):
    def each(act):
        for i, a in enumerate((a0, a1, a2, a3, b0, b1, b2, b3)):
            for q in range(JOBS):
                entry = i * JOBS + q
                worker = table[entry]

                @pl.when(worker >= 0)
                def _():
                    act(pltpu.make_async_copy(a.at[q, 0:PIECE], out.at[worker], sems.at[entry]))

    each(lambda copy: copy.start())
    each(lambda copy: copy.wait())


def select_kernel(table, got, out, sems):
    copies = [
        pltpu.make_async_copy(got.at[table[OWNER_AT + j]], out.at[j], sems.at[j])
        for j in range(WORK_DEV)
    ]
    for copy in copies:
        copy.start()
    for copy in copies:
        copy.wait()


def span_kernel(table, a0, a1, a2, a3, b0, b1, b2, b3, out):
    out[...] = jnp.zeros(out.shape, f32)
    for i, a in enumerate((a0, a1, a2, a3, b0, b1, b2, b3)):
        for q in range(JOBS):
            s = table[SLOT_AT + i * JOBS + q]

            @pl.when(s >= 0)
            def _():
                block = a[q, PIECE:SENT, :].astype(f32)
                off = (s & 3) * BLOCK
                out[s >> 2, :, pl.ds(pl.multiple_of(off, 128), 128)] = block[0:MEL]
                out[s >> 2, :, pl.ds(pl.multiple_of(off + 128, 128), 128)] = block[MEL : 2 * MEL]


def final_kernel(b0, b1, b2, b3, out, stage):
    m = lax.axis_index("mp")
    for k, b in enumerate((b0, b1, b2, b3)):
        quarter = (m - k) & 3
        at = pl.multiple_of(quarter * PIECE, 16)
        for j in range(WORK_DEV):
            stage[j, pl.ds(at, PIECE), :] = b[j]
    for j in range(WORK_DEV):
        out[j, :, 0:128] = stage[j, 0:MEL, :].astype(f32)
        out[j, :, 128:256] = stage[j, MEL : 2 * MEL, :].astype(f32)


def call(kernel, outs, kinds, args, scratch=(), out_kinds=None, limit=24):
    spaces = {"s": SMEM, "v": VMEM, "h": pl.ANY}
    spec = lambda kind: pl.BlockSpec(memory_space=spaces[kind])
    many = isinstance(outs, tuple)
    out_kinds = out_kinds or "v" * (len(outs) if many else 1)
    out_specs = tuple(spec(k) for k in out_kinds)
    return pl.pallas_call(
        kernel,
        out_shape=outs,
        in_specs=[spec(k) for k in kinds],
        out_specs=out_specs if many else out_specs[0],
        scratch_shapes=list(scratch),
        compiler_params=pltpu.CompilerParams(vmem_limit_bytes=limit * 1024 * 1024),
    )(*args)


def shape(dims, dtype):
    return jax.ShapeDtypeStruct(dims, dtype)


def to_next(value, k):
    return lax.ppermute(value, "mp", [(i, (i + k) % N_MP) for i in range(N_MP)])


def to_other(value):
    size = lax.axis_size("dp")
    return lax.ppermute(value, "dp", [(i, i ^ 1) for i in range(size)])


def gathered(value):
    return [value] + [to_next(value, k) for k in range(1, N_MP)]


def after(value, *others):
    return lax.optimization_barrier((value, *others))[0]


def run_plan(plan, audio, w_input, e_rows):
    return call(
        plan_kernel,
        (
            shape((TABLE,), jnp.int32),
            shape((2 * ROWS, ROWS), bf16),
            shape((JOBS, MEL, WIN), bf16),
            shape((JOBS, MEL, BLOCK), bf16),
            shape((JOBS, 8, WIN), f32),
            shape((JOBS, ROWS, BLOCK), bf16),
            shape((JOBS, ROWS, WIN), bf16),
            shape((JOBS, WIN, ROWS), bf16),
            shape((JOBS, ROWS, BLOCK), bf16),
        ),
        "sss" + "v" * 7,
        (*plan, *audio, w_input, e_rows, plan[0].reshape(4, 128)),
        scratch=[VMEM((MEL, 640), bf16), VMEM((MEL, BLOCK), bf16)],
        out_kinds="s" + "v" * 8,
    )


def run_first(table, windows, wp):
    return call(
        first_kernel,
        (
            shape((D, ROWS), bf16),
            shape((D, ROWS), bf16),
            shape((ROWS, D), bf16),
            shape((JOBS, D + ROWS, BLOCK), bf16),
        ),
        "s" + "v" * 12,
        (table, *windows, *wp),
        scratch=work_shapes(),
        limit=MAIN_LIMIT,
    )


def work_shapes():
    return [VMEM((4, WIN, 256), bf16), VMEM((D, BLOCK), bf16), VMEM((D, WIN), bf16)]


def run_second(table, context, noise, valid, gram, first, wa_t, wm, wo):
    return call(
        second_kernel,
        (shape((JOBS, SENT, 128), bf16),) * 4,
        "s" + "v" * 17,
        (table, context, noise, valid, gram, *first, wa_t, wm, *wo),
        scratch=work_shapes()
        + [
            VMEM((D + ROWS, BLOCK), bf16),
            VMEM((D + MEL, D + ROWS), bf16),
            VMEM((4 * PIECE, 128), bf16),
            VMEM((ROWS, BLOCK), bf16),
            VMEM((ROWS, WIN), bf16),
            VMEM((WIN, ROWS), bf16),
        ],
        limit=MAIN_LIMIT,
    )


def shards(
    mel_audio, start_noise, span_start, span_length, block_route,
    w_input, attn_gain, w_qkv, w_out, final_gain, w_mel,
):
    e_rows = jnp.asarray(time_rows())
    plan = (block_route, span_start, span_length)
    w3 = jnp.transpose(w_qkv, (1, 0, 2))
    whole, half = call(
        fold_kernel,
        (shape((3, ROWS, 256), bf16), shape((3, ROWS, 128), bf16)),
        "hhhh",
        (w_input, e_rows, attn_gain.reshape(1, D), w3),
        scratch=[
            VMEM((2 * MEL, D), bf16),
            VMEM((16, D), f32),
            VMEM((1, D), f32),
            VMEM((3, D, 256), bf16),
            pltpu.SemaphoreType.DMA((6,)),
        ],
        limit=60,
    )
    halves = gathered(half)[1:]
    mel_late, noise_late = after(mel_audio, half), after(start_noise, half)
    audio = (mel_audio, to_other(mel_late), start_noise, to_other(noise_late))
    table, gram, context, noise, valid, scaled, values, keys, own_win = run_plan(
        plan, audio, w_input, e_rows
    )
    wa_t, wo_t, wo_half, wm = call(
        prep_kernel,
        (
            shape((D, ROWS), bf16),
            shape((D, 256), bf16),
            shape((D, 128), bf16),
            shape((MEL, D), bf16),
        ),
        "vvvvv",
        (w_input, e_rows, after(w_out, table), w_mel, final_gain.reshape(1, D)),
    )
    out_halves = gathered(wo_half)[1:]
    *halves, _ = lax.optimization_barrier((*halves, wo_half))
    wp = [whole]
    for h in halves:
        wp += [h, to_other(h)]
    first = run_first(table, (valid, scaled, values, keys, own_win), wp)
    out_halves = lax.optimization_barrier((*out_halves, first[3]))
    first = (*first[:3], out_halves[-1])
    wo = [wo_t]
    for h in out_halves[:-1]:
        wo += [h, to_other(h)]
    v0, v1, v2, v3 = run_second(table, context, noise, valid, gram, first, wa_t, wm, wo)
    pieces = [v0] + [to_next(v, k) for k, v in ((1, v1), (2, v2), (3, v3))]
    pieces += [to_other(v) for v in pieces]
    packed = call(
        pack_kernel,
        shape((32, PIECE, 128), bf16),
        "s" + "h" * 8,
        (table, *pieces),
        scratch=[pltpu.SemaphoreType.DMA((8 * JOBS,))],
        out_kinds="h",
    )
    got = lax.all_to_all(packed, "dp", 0, 0, tiled=True)
    infilled = call(
        span_kernel, shape((UTT_DEV, MEL, SPAN_MAX), f32), "s" + "v" * 8, (table, *pieces)
    )
    table, infilled = lax.optimization_barrier((table, infilled))
    chosen = call(
        select_kernel,
        shape((WORK_DEV, PIECE, 128), bf16),
        "sh",
        (table, got),
        scratch=[pltpu.SemaphoreType.DMA((WORK_DEV,))],
        out_kinds="h",
    )
    parts = gathered(chosen)
    velocity = call(
        final_kernel,
        shape((WORK_DEV, MEL, BLOCK), f32),
        "vvvv",
        tuple(parts),
        scratch=[VMEM((WORK_DEV, 4 * PIECE, 128), bf16)],
    )
    return (infilled, velocity)


def solution(mesh):
    return jax.shard_map(
        shards,
        mesh=mesh,
        in_specs=(
            P("dp", None, None),
            P("dp", None, None),
            P(),
            P(),
            P(),
            P(),
            P(),
            P(None, None, "mp"),
            P("mp", None),
            P(),
            P(),
        ),
        out_specs=(P("dp", None, None), P("dp", None, None)),
        check_vma=False,
    )
```

```python
import math

import jax
import jax.numpy as jnp
import numpy as np
from jax import lax
from jax.experimental import pallas as pl
from jax.experimental.pallas import tpu as pltpu
from jax.sharding import PartitionSpec as P

D = 1024
MEL = 80
HEAD_DIM = 64
HEADS = 16
BLOCK = 256
CTX = 128
BLK_UTT = 4
UTT_DEV = 4
WORK_DEV = 6
EULER = 2
FRAMES = 2048
WIN = 512
SPAN_MAX = 1024
SLOT_DEV = 16
N_MP = 4
JOBS = 4
ROWS = 176
PIECE = 48
flow_steps = 32.0
norm_eps = 1e-05
f32 = jnp.float32
bf16 = jnp.bfloat16
VMEM = pltpu.VMEM
SMEM = pltpu.SMEM
MAIN_LIMIT = 44
SLOT_AT, JOB_AT, COUNT_AT, OWNER_AT, TABLE = 32, 64, 68, 72, 80


def time_rows():
    half = D // 2
    freqs = np.exp(-math.log(10000.0) * np.arange(half, dtype=np.float32) / half)
    rows = np.zeros((16, D), np.float32)
    for step in range(EULER):
        angles = np.float32(1000.0 * step / flow_steps) * freqs.astype(np.float32)
        e = np.concatenate([np.sin(angles), np.cos(angles)])
        e = e - e.mean()
        rows[2 * step] = e
        rows[2 * step + 1] = e
    return rows


def high_low(rows):
    high = rows.astype(bf16).astype(f32)
    odd = lax.broadcasted_iota(jnp.int32, rows.shape, 0) % 2 == 1
    return jnp.where(odd, rows - high, high)


def fold_kernel(w_in_h, e_rows_h, gain_h, w_qkv_h, out, half, w_in, e_rows, gain, w_qkv, sems):
    pairs = [(w_in_h, w_in), (e_rows_h, e_rows), (gain_h, gain)]
    pairs += [(w_qkv_h.at[c], w_qkv.at[c]) for c in range(3)]
    copies = [pltpu.make_async_copy(a, b, sems.at[i]) for i, (a, b) in enumerate(pairs)]
    for copy in copies:
        copy.start()
    for copy in copies[0:3]:
        copy.wait()
    core = lax.axis_index("dp") & 1
    w = w_in[...].astype(f32)
    wc = w - jnp.mean(w, axis=1, keepdims=True)
    g = gain[...]
    wag = jnp.concatenate([wc * g, high_low(e_rows[...] * g)], axis=0).astype(bf16)
    for c in range(3):
        copies[3 + c].wait()
        res = jnp.dot(wag, w_qkv[c], preferred_element_type=f32)
        if c == 0:
            res = res * (math.log2(math.e) / math.sqrt(HEAD_DIM))
        e_res = res[160:176]
        row = lax.broadcasted_iota(jnp.int32, e_res.shape, 0)
        first = e_res[0:1] + e_res[1:2]
        second = e_res[2:3] + e_res[3:4]
        both = jnp.where(row < 2, first, jnp.where(row < 4, second, 0.0))
        out[c, 0:160, :] = res[0:160].astype(bf16)
        out[c, 160:176, :] = high_low(both).astype(bf16)
        half[c] = jnp.where(core == 0, out[c, :, 0:128], out[c, :, 128:256])


def prep_kernel(w_in, e_rows, w_out, w_mel, gain, wa_t, wo_t, half, wm):
    w = w_in[...].astype(f32)
    wc = w - jnp.mean(w, axis=1, keepdims=True)
    wa = jnp.concatenate([wc, high_low(e_rows[...]), jnp.zeros((80, D), f32)], axis=0)
    wa_t[...] = wa.T[:, :ROWS].astype(bf16)
    core = lax.axis_index("dp") & 1
    o = w_out[...].astype(f32)
    o = o - jnp.mean(o, axis=1, keepdims=True)
    wo_t[...] = o.T.astype(bf16)
    half[...] = jnp.where(core == 0, wo_t[:, 0:128], wo_t[:, 128:256])
    wm[...] = (w_mel[...].astype(f32) * gain[...]).astype(bf16)


def plan_kernel(
    route, starts, lengths, mel_a, mel_b, noise_a, noise_b, w_in, e_rows, route_v,
    table, gram, context_out, noise_out, valid_out, scaled_out, values_out, keys_out, own_out,
    chunk_s, x_s,
):
    dp = lax.axis_index("dp")
    m = lax.axis_index("mp")
    core = dp & 1
    w = w_in[...].astype(f32)
    wc = w - jnp.mean(w, axis=1, keepdims=True)
    wa = jnp.concatenate([wc, high_low(e_rows[...]), jnp.zeros((80, D), f32)], axis=0)
    wab = wa.astype(bf16)
    g = lax.dot_general(wab, wab, (((1,), (1,)), ((), ())), preferred_element_type=f32)
    g = g[0:ROWS, 0:ROWS] * (1.0 / D)
    high = g.astype(bf16)
    gram[0:ROWS, :] = high
    gram[ROWS : 2 * ROWS, :] = (g - high.astype(f32)).astype(bf16)
    base = (dp >> 1) * (2 * SLOT_DEV)
    seat = core * N_MP + m
    for i in range(TABLE):
        table[i] = -1

    def scan(s, rank):
        dest = route[base + s]
        live = dest >= 0
        q = rank >> 3

        @pl.when(jnp.logical_and(live, (rank & 7) == seat))
        def _():
            table[JOB_AT + q] = s

        @pl.when(jnp.logical_and(live, (s >> 4) == core))
        def _():
            away = ((rank >> 2) & 1) ^ core
            entry = (away * 4 + ((m - rank) & 3)) * JOBS + q
            table[entry] = (dest * 10923) >> 16
            table[SLOT_AT + entry] = s & 15

        return rank + live.astype(jnp.int32)

    n_live = lax.fori_loop(0, 2 * SLOT_DEV, scan, jnp.int32(0))
    n_jobs = (n_live - seat + 7) >> 3
    table[COUNT_AT] = n_jobs

    places = route_v[...]
    owner = (
        lax.broadcasted_iota(jnp.int32, places.shape, 0) * places.shape[1]
        + lax.broadcasted_iota(jnp.int32, places.shape, 1)
    ) >> 4
    for j in range(WORK_DEV):
        found = jnp.where(places == dp * WORK_DEV + j, owner, 0)
        table[OWNER_AT + j] = jnp.sum(found)

    def job(q, carry):
        s = table[JOB_AT + q]
        u = (s >> 2) & 3
        order = s & 3
        utter = (dp >> 1) * (2 * UTT_DEV) + (s >> 2)
        span = starts[utter]
        length = lengths[utter]
        first = span + BLOCK * order - CTX
        aligned = pl.multiple_of(jnp.clip((first >> 7) << 7, 0, FRAMES - 640), 128)
        off = pl.multiple_of(order * BLOCK, BLOCK)
        here = (s >> 4) == core

        @pl.when(here)
        def _():
            chunk_s[...] = mel_a[u, :, pl.ds(aligned, 640)]
            x_s[...] = noise_a[u, :, pl.ds(off, BLOCK)]

        @pl.when(jnp.logical_not(here))
        def _():
            chunk_s[...] = mel_b[u, :, pl.ds(aligned, 640)]
            x_s[...] = noise_b[u, :, pl.ds(off, BLOCK)]

        own = lax.broadcasted_iota(jnp.int32, (1, BLOCK), 1) < length - BLOCK * order
        x = jnp.where(own, x_s[...].astype(f32), 0.0)
        noise_out[q] = x.astype(bf16)
        shift = aligned - first
        shift = jnp.where(shift < 0, shift + 640, shift)
        chunk = pltpu.roll(chunk_s[...].astype(f32), shift, 1)[:, :WIN]
        pos = first + lax.broadcasted_iota(jnp.int32, (1, WIN), 1)
        valid = jnp.logical_and(pos >= 0, pos < FRAMES)
        in_span = jnp.logical_and(pos >= span, pos < span + length)
        keep = jnp.logical_and(valid, jnp.logical_not(in_span))
        context = jnp.where(keep, chunk, 0.0)
        context_out[q] = context.astype(bf16)
        valid = valid.astype(f32)
        in_block = jnp.logical_and(pos >= first + CTX, jnp.logical_and(pos < first + CTX + BLOCK, in_span))
        row = lax.broadcasted_iota(jnp.int32, (8, WIN), 0)
        valid_out[q] = jnp.where(row == 0, valid, in_block.astype(f32))
        window(0, context, valid, x, gram, scaled_out.at[q], values_out.at[q], keys_out.at[q], own_out.at[q])
        return carry

    lax.fori_loop(0, n_jobs, job, 0)


def window(n, context, valid, x, gram, scaled_out, values_out, keys_out, own_out):
    side = jnp.zeros((MEL, CTX), f32)
    state = jnp.concatenate([side, x.astype(bf16).astype(f32), side], axis=1)
    flags = (lax.broadcasted_iota(jnp.int32, (16, WIN), 0) >> 1) == n
    win = jnp.concatenate([context, state, flags.astype(f32)], axis=0)
    win = jnp.where(valid > 0.0, win, win[:, CTX : CTX + 1])
    win_b = win.astype(bf16)
    own_out[...] = win_b[:, CTX : CTX + BLOCK]
    gw = jnp.dot(gram[...], win_b, preferred_element_type=f32)
    var = jnp.sum(win * (gw[0:ROWS] + gw[ROWS : 2 * ROWS]), axis=0, keepdims=True)
    scaled = win * lax.rsqrt(jnp.maximum(var, 0.0) + norm_eps)
    scaled_out[...] = scaled[:, CTX : CTX + BLOCK].astype(bf16)
    values_out[...] = (scaled * valid).astype(bf16)
    padded = jnp.concatenate([scaled, jnp.zeros((256 - ROWS, WIN), f32)], axis=0)
    keys_out[...] = padded.T.astype(bf16)[:, :ROWS]


def attend(scaled, values, win_t, valid, weights, work, o_out):
    wq_s, wv_s, wk_s = weights
    k_s, q_s, v_s = work
    q_s[...] = jnp.dot(wq_s[...], scaled[...], preferred_element_type=f32).astype(bf16)
    keys = jnp.dot(win_t[...], wk_s[...], preferred_element_type=f32).astype(bf16)
    for p in range(4):
        k_s[p] = keys[:, 256 * p : 256 * p + 256]
    v_s[...] = jnp.dot(wv_s[...], values[...], preferred_element_type=f32).astype(bf16)
    ones_rows = jnp.broadcast_to(valid, (16, WIN)).astype(bf16)
    zero = jnp.zeros((HEAD_DIM, BLOCK), bf16)

    def score(g):
        columns = []
        for j in range(4):
            at = 256 * g + 64 * j
            rows = [q_s[at : at + 64, :] if t == j else zero for t in range(4)]
            columns.append(jnp.concatenate(rows, axis=0))
        return jnp.dot(k_s[g], jnp.concatenate(columns, axis=1), preferred_element_type=f32)

    ahead = score(0)
    for g in range(4):
        sc = ahead
        if g < 3:
            ahead = score(g + 1)
        top = jnp.max(sc, axis=0, keepdims=True)
        pr = jnp.exp2(sc - top).astype(bf16)
        for j in range(4):
            at = 256 * g + 64 * j
            lhs = jnp.concatenate([v_s[at : at + 64, :], ones_rows], axis=0)
            ov = jnp.dot(lhs, pr[:, 256 * j : 256 * j + 256], preferred_element_type=f32)
            o_out[at : at + 64, :] = (ov[0:64] / ov[64:65]).astype(bf16)


def velocity_of(wr_s, o, own):
    v = jnp.dot(wr_s[D : D + MEL, :], o[...], preferred_element_type=f32)
    squares = jnp.zeros((8, BLOCK), f32)
    part = D // 4
    for i in range(4):
        r = jnp.dot(wr_s[part * i : part * i + part, :], o[...], preferred_element_type=f32)
        squares = squares + jnp.sum((r * r).reshape(part // 8, 8, BLOCK), axis=0)
    var = jnp.sum(squares, axis=0, keepdims=True) * (1.0 / D)
    return jnp.where(own, v * lax.rsqrt(var + norm_eps), 0.0)


def first_kernel(
    table, valid, scaled, values, keys, own_win,
    wp0, hp1, sp1, hp2, sp2, hp3, sp3,
    wq_s, wv_s, wk_s, o_out,
    k_s, q_s, v_s,
):
    at = 0
    for wp in (wp0, hp1, sp1, hp2, sp2, hp3, sp3):
        width = wp.shape[2]
        lanes = slice(at, at + width)
        pad = jnp.zeros((256 - ROWS, width), f32)
        wq_s[lanes, :] = jnp.concatenate([wp[0].astype(f32), pad], axis=0).T.astype(bf16)[:, :ROWS]
        wv_s[lanes, :] = jnp.concatenate([wp[2].astype(f32), pad], axis=0).T.astype(bf16)[:, :ROWS]
        wk_s[:, lanes] = wp[1]
        at += width

    def job(q, carry):
        o = o_out.at[q]
        o[1024 : 1024 + ROWS, :] = own_win[q]
        attend(
            scaled.at[q], values.at[q], keys.at[q], valid[q, 0:1, :],
            (wq_s, wv_s, wk_s), (k_s, q_s, v_s), o,
        )
        return carry

    lax.fori_loop(0, table[COUNT_AT], job, 0)


def second_kernel(
    table, context, noise, valid, gram, wq_s, wv_s, wk_s, o_in, wa_t, wm,
    wo0, ho1, so1, ho2, so2, ho3, so3,
    tot_out, v0, v1, v2, v3,
    k_s, q_s, v_s, o_s, wr_s, stage, scaled_s, values_s, keys_s,
):
    m = lax.axis_index("mp")
    at = 0
    for wo in (wo0, ho1, so1, ho2, so2, ho3, so3):
        width = wo.shape[1]
        wr_s[0:D, at : at + width] = wo[...]
        at += width
    wr_s[0:D, 1024 : 1024 + ROWS] = wa_t[...]
    wr_s[D : D + MEL, :] = jnp.dot(wm[...], wr_s[0:D, :], preferred_element_type=f32).astype(bf16)
    stage[...] = jnp.zeros(stage.shape, bf16)

    def job(q, carry):
        masks = valid[q]
        own = masks[1:2, CTX : CTX + BLOCK] > 0.0
        usable = masks[0:1, :]
        first = velocity_of(wr_s, o_in.at[q], own)
        x = noise[q].astype(f32) + first * (1.0 / flow_steps)
        window(
            1, context[q].astype(f32), usable, x, gram,
            scaled_s, values_s, keys_s, o_s.at[1024 : 1024 + ROWS, :],
        )
        attend(
            scaled_s, values_s, keys_s, usable, (wq_s, wv_s, wk_s), (k_s, q_s, v_s), o_s
        )
        last = velocity_of(wr_s, o_s, own)
        total = (first + last).astype(bf16)
        tot_out[q, 0:MEL, :] = total[:, 0:128]
        tot_out[q, MEL : 2 * MEL, :] = total[:, 128:256]
        vel = last.astype(bf16)
        stage[0:MEL, :] = vel[:, 0:128]
        stage[MEL : 2 * MEL, :] = vel[:, 128:256]
        for k, out in enumerate((v0, v1, v2, v3)):
            quarter = (m + k) & 3
            out[q] = stage[pl.ds(pl.multiple_of(quarter * PIECE, 16), PIECE), :]
        return carry

    lax.fori_loop(0, table[COUNT_AT], job, 0)


def pack_kernel(table, a0, a1, a2, a3, b0, b1, b2, b3, out, sems):
    def each(act):
        for i, a in enumerate((a0, a1, a2, a3, b0, b1, b2, b3)):
            for q in range(JOBS):
                entry = i * JOBS + q
                worker = table[entry]

                @pl.when(worker >= 0)
                def _():
                    act(pltpu.make_async_copy(a.at[q], out.at[worker], sems.at[entry]))

    each(lambda copy: copy.start())
    each(lambda copy: copy.wait())


def select_kernel(table, got, out, sems):
    copies = [
        pltpu.make_async_copy(got.at[table[OWNER_AT + j]], out.at[j], sems.at[j])
        for j in range(WORK_DEV)
    ]
    for copy in copies:
        copy.start()
    for copy in copies:
        copy.wait()


def span_kernel(table, a0, a1, a2, a3, b, out):
    out[...] = jnp.zeros(out.shape, f32)
    sources = [lambda q, a=a: a[q] for a in (a0, a1, a2, a3)]
    sources += [lambda q, k=k: b[k * JOBS + q] for k in range(N_MP)]
    for i, source in enumerate(sources):
        for q in range(JOBS):
            s = table[SLOT_AT + i * JOBS + q]

            @pl.when(s >= 0)
            def _():
                block = source(q).astype(f32)
                off = (s & 3) * BLOCK
                out[s >> 2, :, pl.ds(pl.multiple_of(off, 128), 128)] = block[0:MEL]
                out[s >> 2, :, pl.ds(pl.multiple_of(off + 128, 128), 128)] = block[MEL : 2 * MEL]


def final_kernel(b0, b1, b2, b3, out, stage):
    m = lax.axis_index("mp")
    for k, b in enumerate((b0, b1, b2, b3)):
        quarter = (m - k) & 3
        at = pl.multiple_of(quarter * PIECE, 16)
        for j in range(WORK_DEV):
            stage[j, pl.ds(at, PIECE), :] = b[j]
    for j in range(WORK_DEV):
        out[j, :, 0:128] = stage[j, 0:MEL, :].astype(f32)
        out[j, :, 128:256] = stage[j, MEL : 2 * MEL, :].astype(f32)


def call(kernel, outs, kinds, args, scratch=(), out_kinds=None, limit=24):
    spaces = {"s": SMEM, "v": VMEM, "h": pl.ANY}
    spec = lambda kind: pl.BlockSpec(memory_space=spaces[kind])
    many = isinstance(outs, tuple)
    out_kinds = out_kinds or "v" * (len(outs) if many else 1)
    out_specs = tuple(spec(k) for k in out_kinds)
    return pl.pallas_call(
        kernel,
        out_shape=outs,
        in_specs=[spec(k) for k in kinds],
        out_specs=out_specs if many else out_specs[0],
        scratch_shapes=list(scratch),
        compiler_params=pltpu.CompilerParams(vmem_limit_bytes=limit * 1024 * 1024),
    )(*args)


def shape(dims, dtype):
    return jax.ShapeDtypeStruct(dims, dtype)


def to_next(value, k):
    return lax.ppermute(value, "mp", [(i, (i + k) % N_MP) for i in range(N_MP)])


def to_other(value):
    size = lax.axis_size("dp")
    return lax.ppermute(value, "dp", [(i, i ^ 1) for i in range(size)])


def gathered(value):
    return [value] + [to_next(value, k) for k in range(1, N_MP)]


def after(value, *others):
    return lax.optimization_barrier((value, *others))[0]


def run_plan(plan, audio, w_input, e_rows):
    return call(
        plan_kernel,
        (
            shape((TABLE,), jnp.int32),
            shape((2 * ROWS, ROWS), bf16),
            shape((JOBS, MEL, WIN), bf16),
            shape((JOBS, MEL, BLOCK), bf16),
            shape((JOBS, 8, WIN), f32),
            shape((JOBS, ROWS, BLOCK), bf16),
            shape((JOBS, ROWS, WIN), bf16),
            shape((JOBS, WIN, ROWS), bf16),
            shape((JOBS, ROWS, BLOCK), bf16),
        ),
        "sss" + "v" * 7,
        (*plan, *audio, w_input, e_rows, plan[0].reshape(4, 128)),
        scratch=[VMEM((MEL, 640), bf16), VMEM((MEL, BLOCK), bf16)],
        out_kinds="s" + "v" * 8,
    )


def run_first(table, windows, wp):
    return call(
        first_kernel,
        (
            shape((D, ROWS), bf16),
            shape((D, ROWS), bf16),
            shape((ROWS, D), bf16),
            shape((JOBS, D + ROWS, BLOCK), bf16),
        ),
        "s" + "v" * 12,
        (table, *windows, *wp),
        scratch=work_shapes(),
        limit=MAIN_LIMIT,
    )


def work_shapes():
    return [VMEM((4, WIN, 256), bf16), VMEM((D, BLOCK), bf16), VMEM((D, WIN), bf16)]


def run_second(table, context, noise, valid, gram, first, wa_t, wm, wo):
    return call(
        second_kernel,
        (shape((JOBS, 2 * MEL, 128), bf16),) + (shape((JOBS, PIECE, 128), bf16),) * 4,
        "s" + "v" * 17,
        (table, context, noise, valid, gram, *first, wa_t, wm, *wo),
        scratch=work_shapes()
        + [
            VMEM((D + ROWS, BLOCK), bf16),
            VMEM((D + MEL, D + ROWS), bf16),
            VMEM((4 * PIECE, 128), bf16),
            VMEM((ROWS, BLOCK), bf16),
            VMEM((ROWS, WIN), bf16),
            VMEM((WIN, ROWS), bf16),
        ],
        limit=MAIN_LIMIT,
    )


def shards(
    mel_audio, start_noise, span_start, span_length, block_route,
    w_input, attn_gain, w_qkv, w_out, final_gain, w_mel,
):
    e_rows = jnp.asarray(time_rows())
    plan = (block_route, span_start, span_length)
    w3 = jnp.transpose(w_qkv, (1, 0, 2))
    whole, half = call(
        fold_kernel,
        (shape((3, ROWS, 256), bf16), shape((3, ROWS, 128), bf16)),
        "hhhh",
        (w_input, e_rows, attn_gain.reshape(1, D), w3),
        scratch=[
            VMEM((2 * MEL, D), bf16),
            VMEM((16, D), f32),
            VMEM((1, D), f32),
            VMEM((3, D, 256), bf16),
            pltpu.SemaphoreType.DMA((6,)),
        ],
        limit=60,
    )
    halves = gathered(half)[1:]
    mel_late, noise_late = after(mel_audio, half), after(start_noise, half)
    audio = (mel_audio, to_other(mel_late), start_noise, to_other(noise_late))
    table, gram, context, noise, valid, scaled, values, keys, own_win = run_plan(
        plan, audio, w_input, e_rows
    )
    wa_t, wo_t, wo_half, wm = call(
        prep_kernel,
        (
            shape((D, ROWS), bf16),
            shape((D, 256), bf16),
            shape((D, 128), bf16),
            shape((MEL, D), bf16),
        ),
        "vvvvv",
        (w_input, e_rows, after(w_out, table), w_mel, final_gain.reshape(1, D)),
    )
    out_halves = gathered(wo_half)[1:]
    *halves, _ = lax.optimization_barrier((*halves, wo_half))
    wp = [whole]
    for h in halves:
        wp += [h, to_other(h)]
    first = run_first(table, (valid, scaled, values, keys, own_win), wp)
    out_halves = lax.optimization_barrier((*out_halves, first[3]))
    first = (*first[:3], out_halves[-1])
    wo = [wo_t]
    for h in out_halves[:-1]:
        wo += [h, to_other(h)]
    tot, v0, v1, v2, v3 = run_second(table, context, noise, valid, gram, first, wa_t, wm, wo)
    pieces = [v0] + [to_next(v, k) for k, v in ((1, v1), (2, v2), (3, v3))]
    totals = gathered(after(tot, *pieces[1:]))
    pieces += [to_other(v) for v in pieces]
    packed = call(
        pack_kernel,
        shape((32, PIECE, 128), bf16),
        "s" + "h" * 8,
        (table, *pieces),
        scratch=[pltpu.SemaphoreType.DMA((8 * JOBS,))],
        out_kinds="h",
    )
    got = lax.all_to_all(packed, "dp", 0, 0, tiled=True)
    chosen = call(
        select_kernel,
        shape((WORK_DEV, PIECE, 128), bf16),
        "sh",
        (table, got),
        scratch=[pltpu.SemaphoreType.DMA((WORK_DEV,))],
        out_kinds="h",
    )
    parts = gathered(chosen)
    *totals, _ = lax.optimization_barrier((*totals, chosen))
    infilled = call(
        span_kernel,
        shape((UTT_DEV, MEL, SPAN_MAX), f32),
        "s" + "v" * 5,
        (table, *totals, to_other(jnp.concatenate(totals, axis=0))),
    )
    *parts, infilled = lax.optimization_barrier((*parts, infilled))
    velocity = call(
        final_kernel,
        shape((WORK_DEV, MEL, BLOCK), f32),
        "vvvv",
        tuple(parts),
        scratch=[VMEM((WORK_DEV, 4 * PIECE, 128), bf16)],
    )
    return (infilled, velocity)


def solution(mesh):
    return jax.shard_map(
        shards,
        mesh=mesh,
        in_specs=(
            P("dp", None, None),
            P("dp", None, None),
            P(),
            P(),
            P(),
            P(),
            P(),
            P(None, None, "mp"),
            P("mp", None),
            P(),
            P(),
        ),
        out_specs=(P("dp", None, None), P("dp", None, None)),
        check_vma=False,
    )
```

```python
import math

import jax
import jax.numpy as jnp
import numpy as np
from jax import lax
from jax.experimental import pallas as pl
from jax.experimental.pallas import tpu as pltpu
from jax.sharding import PartitionSpec as P

D = 1024
MEL = 80
HEAD_DIM = 64
HEADS = 16
BLOCK = 256
CTX = 128
BLK_UTT = 4
UTT_DEV = 4
WORK_DEV = 6
EULER = 2
FRAMES = 2048
WIN = 512
SPAN_MAX = 1024
SLOT_DEV = 16
N_MP = 4
JOBS = 4
ROWS = 176
PIECE = 48
flow_steps = 32.0
norm_eps = 1e-05
f32 = jnp.float32
bf16 = jnp.bfloat16
VMEM = pltpu.VMEM
SMEM = pltpu.SMEM
MAIN_LIMIT = 44
SLOT_AT, JOB_AT, COUNT_AT, OWNER_AT, TABLE = 32, 64, 68, 72, 80


def time_rows():
    half = D // 2
    freqs = np.exp(-math.log(10000.0) * np.arange(half, dtype=np.float32) / half)
    rows = np.zeros((16, D), np.float32)
    for step in range(EULER):
        angles = np.float32(1000.0 * step / flow_steps) * freqs.astype(np.float32)
        e = np.concatenate([np.sin(angles), np.cos(angles)])
        e = e - e.mean()
        rows[2 * step] = e
        rows[2 * step + 1] = e
    return rows


def high_low(rows):
    high = rows.astype(bf16).astype(f32)
    odd = lax.broadcasted_iota(jnp.int32, rows.shape, 0) % 2 == 1
    return jnp.where(odd, rows - high, high)


def fold_kernel(w_in_h, e_rows_h, gain_h, w_qkv_h, out, half, w_in, e_rows, gain, w_qkv, sems):
    pairs = [(w_in_h, w_in), (e_rows_h, e_rows), (gain_h, gain)]
    pairs += [(w_qkv_h.at[c], w_qkv.at[c]) for c in range(3)]
    copies = [pltpu.make_async_copy(a, b, sems.at[i]) for i, (a, b) in enumerate(pairs)]
    for copy in copies:
        copy.start()
    for copy in copies[0:3]:
        copy.wait()
    core = lax.axis_index("dp") & 1
    w = w_in[...].astype(f32)
    wc = w - jnp.mean(w, axis=1, keepdims=True)
    g = gain[...]
    wag = jnp.concatenate([wc * g, high_low(e_rows[...] * g)], axis=0).astype(bf16)
    for c in range(3):
        copies[3 + c].wait()
        res = jnp.dot(wag, w_qkv[c], preferred_element_type=f32)
        if c == 0:
            res = res * (math.log2(math.e) / math.sqrt(HEAD_DIM))
        e_res = res[160:176]
        row = lax.broadcasted_iota(jnp.int32, e_res.shape, 0)
        first = e_res[0:1] + e_res[1:2]
        second = e_res[2:3] + e_res[3:4]
        both = jnp.where(row < 2, first, jnp.where(row < 4, second, 0.0))
        out[c, 0:160, :] = res[0:160].astype(bf16)
        out[c, 160:176, :] = high_low(both).astype(bf16)
        half[c] = jnp.where(core == 0, out[c, :, 0:128], out[c, :, 128:256])


def prep_kernel(w_in, e_rows, w_out, w_mel, gain, wa_t, wo_t, half, wm):
    w = w_in[...].astype(f32)
    wc = w - jnp.mean(w, axis=1, keepdims=True)
    wa = jnp.concatenate([wc, high_low(e_rows[...]), jnp.zeros((80, D), f32)], axis=0)
    wa_t[...] = wa.T[:, :ROWS].astype(bf16)
    core = lax.axis_index("dp") & 1
    o = w_out[...].astype(f32)
    o = o - jnp.mean(o, axis=1, keepdims=True)
    wo_t[...] = o.T.astype(bf16)
    half[...] = jnp.where(core == 0, wo_t[:, 0:128], wo_t[:, 128:256])
    wm[...] = (w_mel[...].astype(f32) * gain[...]).astype(bf16)


def plan_kernel(
    route, starts, lengths, mel_a, mel_b, noise_a, noise_b, w_in, e_rows, route_v,
    table, gram, context_out, noise_out, valid_out, scaled_out, values_out, keys_out, own_out,
    chunk_s, x_s,
):
    dp = lax.axis_index("dp")
    m = lax.axis_index("mp")
    core = dp & 1
    w = w_in[...].astype(f32)
    wc = w - jnp.mean(w, axis=1, keepdims=True)
    wa = jnp.concatenate([wc, high_low(e_rows[...]), jnp.zeros((80, D), f32)], axis=0)
    wab = wa.astype(bf16)
    g = lax.dot_general(wab, wab, (((1,), (1,)), ((), ())), preferred_element_type=f32)
    g = g[0:ROWS, 0:ROWS] * (1.0 / D)
    high = g.astype(bf16)
    gram[0:ROWS, :] = high
    gram[ROWS : 2 * ROWS, :] = (g - high.astype(f32)).astype(bf16)
    base = (dp >> 1) * (2 * SLOT_DEV)
    seat = core * N_MP + m
    for i in range(TABLE):
        table[i] = -1

    def scan(s, rank):
        dest = route[base + s]
        live = dest >= 0
        q = rank >> 3

        @pl.when(jnp.logical_and(live, (rank & 7) == seat))
        def _():
            table[JOB_AT + q] = s

        @pl.when(jnp.logical_and(live, (s >> 4) == core))
        def _():
            away = ((rank >> 2) & 1) ^ core
            entry = (away * 4 + ((m - rank) & 3)) * JOBS + q
            table[entry] = (dest * 10923) >> 16
            table[SLOT_AT + entry] = s & 15

        return rank + live.astype(jnp.int32)

    n_live = lax.fori_loop(0, 2 * SLOT_DEV, scan, jnp.int32(0))
    n_jobs = (n_live - seat + 7) >> 3
    table[COUNT_AT] = n_jobs

    places = route_v[...]
    owner = (
        lax.broadcasted_iota(jnp.int32, places.shape, 0) * places.shape[1]
        + lax.broadcasted_iota(jnp.int32, places.shape, 1)
    ) >> 4
    for j in range(WORK_DEV):
        found = jnp.where(places == dp * WORK_DEV + j, owner, 0)
        table[OWNER_AT + j] = jnp.sum(found)

    def job(q, carry):
        s = table[JOB_AT + q]
        u = (s >> 2) & 3
        order = s & 3
        utter = (dp >> 1) * (2 * UTT_DEV) + (s >> 2)
        span = starts[utter]
        length = lengths[utter]
        first = span + BLOCK * order - CTX
        aligned = pl.multiple_of(jnp.clip((first >> 7) << 7, 0, FRAMES - 640), 128)
        off = pl.multiple_of(order * BLOCK, BLOCK)
        here = (s >> 4) == core

        @pl.when(here)
        def _():
            chunk_s[...] = mel_a[u, :, pl.ds(aligned, 640)]
            x_s[...] = noise_a[u, :, pl.ds(off, BLOCK)]

        @pl.when(jnp.logical_not(here))
        def _():
            chunk_s[...] = mel_b[u, :, pl.ds(aligned, 640)]
            x_s[...] = noise_b[u, :, pl.ds(off, BLOCK)]

        own = lax.broadcasted_iota(jnp.int32, (1, BLOCK), 1) < length - BLOCK * order
        x = jnp.where(own, x_s[...].astype(f32), 0.0)
        noise_out[q] = x.astype(bf16)
        shift = aligned - first
        shift = jnp.where(shift < 0, shift + 640, shift)
        chunk = pltpu.roll(chunk_s[...].astype(f32), shift, 1)[:, :WIN]
        pos = first + lax.broadcasted_iota(jnp.int32, (1, WIN), 1)
        valid = jnp.logical_and(pos >= 0, pos < FRAMES)
        in_span = jnp.logical_and(pos >= span, pos < span + length)
        keep = jnp.logical_and(valid, jnp.logical_not(in_span))
        context = jnp.where(keep, chunk, 0.0)
        context_out[q] = context.astype(bf16)
        valid = valid.astype(f32)
        in_block = jnp.logical_and(pos >= first + CTX, jnp.logical_and(pos < first + CTX + BLOCK, in_span))
        row = lax.broadcasted_iota(jnp.int32, (8, WIN), 0)
        valid_out[q] = jnp.where(row == 0, valid, in_block.astype(f32))
        window(0, context, valid, x, gram, scaled_out.at[q], values_out.at[q], keys_out.at[q], own_out.at[q])
        return carry

    lax.fori_loop(0, n_jobs, job, 0)


def window(n, context, valid, x, gram, scaled_out, values_out, keys_out, own_out):
    side = jnp.zeros((MEL, CTX), f32)
    state = jnp.concatenate([side, x.astype(bf16).astype(f32), side], axis=1)
    flags = (lax.broadcasted_iota(jnp.int32, (16, WIN), 0) >> 1) == n
    win = jnp.concatenate([context, state, flags.astype(f32)], axis=0)
    win = jnp.where(valid > 0.0, win, win[:, CTX : CTX + 1])
    win_b = win.astype(bf16)
    own_out[...] = win_b[:, CTX : CTX + BLOCK]
    gw = jnp.dot(gram[...], win_b, preferred_element_type=f32)
    var = jnp.sum(win * (gw[0:ROWS] + gw[ROWS : 2 * ROWS]), axis=0, keepdims=True)
    scaled = win * lax.rsqrt(jnp.maximum(var, 0.0) + norm_eps)
    scaled_out[...] = scaled[:, CTX : CTX + BLOCK].astype(bf16)
    values_out[...] = (scaled * valid).astype(bf16)
    padded = jnp.concatenate([scaled, jnp.zeros((256 - ROWS, WIN), f32)], axis=0)
    keys_out[...] = padded.T.astype(bf16)[:, :ROWS]


def attend(scaled, values, win_t, valid, weights, work, o_out):
    wq_s, wv_s, wk_s = weights
    k_s, q_s, v_s = work
    q_s[...] = jnp.dot(wq_s[...], scaled[...], preferred_element_type=f32).astype(bf16)
    keys = jnp.dot(win_t[...], wk_s[...], preferred_element_type=f32).astype(bf16)
    for p in range(4):
        k_s[p] = keys[:, 256 * p : 256 * p + 256]
    v_s[...] = jnp.dot(wv_s[...], values[...], preferred_element_type=f32).astype(bf16)
    ones_rows = jnp.broadcast_to(valid, (16, WIN)).astype(bf16)
    zero = jnp.zeros((HEAD_DIM, BLOCK), bf16)

    def score(g):
        columns = []
        for j in range(4):
            at = 256 * g + 64 * j
            rows = [q_s[at : at + 64, :] if t == j else zero for t in range(4)]
            columns.append(jnp.concatenate(rows, axis=0))
        return jnp.dot(k_s[g], jnp.concatenate(columns, axis=1), preferred_element_type=f32)

    ahead = score(0)
    for g in range(4):
        sc = ahead
        if g < 3:
            ahead = score(g + 1)
        top = jnp.max(sc, axis=0, keepdims=True)
        pr = jnp.exp2(sc - top).astype(bf16)
        for j in range(4):
            at = 256 * g + 64 * j
            lhs = jnp.concatenate([v_s[at : at + 64, :], ones_rows], axis=0)
            ov = jnp.dot(lhs, pr[:, 256 * j : 256 * j + 256], preferred_element_type=f32)
            o_out[at : at + 64, :] = (ov[0:64] / ov[64:65]).astype(bf16)


def velocity_of(wr_s, o, own):
    squares = jnp.zeros((8, BLOCK), f32)
    part = D // 4
    v = None
    for i in range(4):
        last = i == 3
        rows = slice(part * i, D + MEL if last else part * i + part)
        r = jnp.dot(wr_s[rows, :], o[...], preferred_element_type=f32)
        if last:
            v = r[part:]
            r = r[0:part]
        squares = squares + jnp.sum((r * r).reshape(part // 8, 8, BLOCK), axis=0)
    var = jnp.sum(squares, axis=0, keepdims=True) * (1.0 / D)
    return jnp.where(own, v * lax.rsqrt(var + norm_eps), 0.0)


def first_kernel(
    table, valid, scaled, values, keys, own_win,
    wp0, hp1, sp1, hp2, sp2, hp3, sp3,
    wq_s, wv_s, wk_s, o_out,
    k_s, q_s, v_s,
):
    at = 0
    for wp in (wp0, hp1, sp1, hp2, sp2, hp3, sp3):
        width = wp.shape[2]
        lanes = slice(at, at + width)
        pad = jnp.zeros((256 - ROWS, width), f32)
        wq_s[lanes, :] = jnp.concatenate([wp[0].astype(f32), pad], axis=0).T.astype(bf16)[:, :ROWS]
        wv_s[lanes, :] = jnp.concatenate([wp[2].astype(f32), pad], axis=0).T.astype(bf16)[:, :ROWS]
        wk_s[:, lanes] = wp[1]
        at += width

    def job(q, carry):
        o = o_out.at[q]
        o[1024 : 1024 + ROWS, :] = own_win[q]
        attend(
            scaled.at[q], values.at[q], keys.at[q], valid[q, 0:1, :],
            (wq_s, wv_s, wk_s), (k_s, q_s, v_s), o,
        )
        return carry

    lax.fori_loop(0, table[COUNT_AT], job, 0)


def second_kernel(
    table, context, noise, valid, gram, wq_s, wv_s, wk_s, o_in, wa_t, wm,
    wo0, ho1, so1, ho2, so2, ho3, so3,
    tot_out, v0, v1, v2, v3,
    k_s, q_s, v_s, o_s, wr_s, stage, scaled_s, values_s, keys_s,
):
    m = lax.axis_index("mp")
    at = 0
    for wo in (wo0, ho1, so1, ho2, so2, ho3, so3):
        width = wo.shape[1]
        wr_s[0:D, at : at + width] = wo[...]
        at += width
    wr_s[0:D, 1024 : 1024 + ROWS] = wa_t[...]
    wr_s[D : D + MEL, :] = jnp.dot(wm[...], wr_s[0:D, :], preferred_element_type=f32).astype(bf16)
    stage[...] = jnp.zeros(stage.shape, bf16)

    def job(q, carry):
        masks = valid[q]
        own = masks[1:2, CTX : CTX + BLOCK] > 0.0
        usable = masks[0:1, :]
        first = velocity_of(wr_s, o_in.at[q], own)
        x = noise[q].astype(f32) + first * (1.0 / flow_steps)
        window(
            1, context[q].astype(f32), usable, x, gram,
            scaled_s, values_s, keys_s, o_s.at[1024 : 1024 + ROWS, :],
        )
        attend(
            scaled_s, values_s, keys_s, usable, (wq_s, wv_s, wk_s), (k_s, q_s, v_s), o_s
        )
        last = velocity_of(wr_s, o_s, own)
        total = (first + last).astype(bf16)
        tot_out[q, 0:MEL, :] = total[:, 0:128]
        tot_out[q, MEL : 2 * MEL, :] = total[:, 128:256]
        vel = last.astype(bf16)
        stage[0:MEL, :] = vel[:, 0:128]
        stage[MEL : 2 * MEL, :] = vel[:, 128:256]
        for k, out in enumerate((v0, v1, v2, v3)):
            quarter = (m + k) & 3
            out[q] = stage[pl.ds(pl.multiple_of(quarter * PIECE, 16), PIECE), :]
        return carry

    lax.fori_loop(0, table[COUNT_AT], job, 0)


def pack_kernel(table, a0, a1, a2, a3, b0, b1, b2, b3, out, sems):
    def each(act):
        for i, a in enumerate((a0, a1, a2, a3, b0, b1, b2, b3)):
            for q in range(JOBS):
                entry = i * JOBS + q
                worker = table[entry]

                @pl.when(worker >= 0)
                def _():
                    act(pltpu.make_async_copy(a.at[q], out.at[worker], sems.at[entry]))

    each(lambda copy: copy.start())
    each(lambda copy: copy.wait())


def select_kernel(table, got, out, sems):
    copies = [
        pltpu.make_async_copy(got.at[table[OWNER_AT + j]], out.at[j], sems.at[j])
        for j in range(WORK_DEV)
    ]
    for copy in copies:
        copy.start()
    for copy in copies:
        copy.wait()


def span_kernel(table, a0, a1, a2, a3, b, out):
    out[...] = jnp.zeros(out.shape, f32)
    sources = [lambda q, a=a: a[q] for a in (a0, a1, a2, a3)]
    sources += [lambda q, k=k: b[k * JOBS + q] for k in range(N_MP)]
    for i, source in enumerate(sources):
        for q in range(JOBS):
            s = table[SLOT_AT + i * JOBS + q]

            @pl.when(s >= 0)
            def _():
                block = source(q).astype(f32)
                off = (s & 3) * BLOCK
                out[s >> 2, :, pl.ds(pl.multiple_of(off, 128), 128)] = block[0:MEL]
                out[s >> 2, :, pl.ds(pl.multiple_of(off + 128, 128), 128)] = block[MEL : 2 * MEL]


def final_kernel(b0, b1, b2, b3, out, stage):
    m = lax.axis_index("mp")
    for k, b in enumerate((b0, b1, b2, b3)):
        quarter = (m - k) & 3
        at = pl.multiple_of(quarter * PIECE, 16)
        for j in range(WORK_DEV):
            stage[j, pl.ds(at, PIECE), :] = b[j]
    for j in range(WORK_DEV):
        out[j, :, 0:128] = stage[j, 0:MEL, :].astype(f32)
        out[j, :, 128:256] = stage[j, MEL : 2 * MEL, :].astype(f32)


def call(kernel, outs, kinds, args, scratch=(), out_kinds=None, limit=24):
    spaces = {"s": SMEM, "v": VMEM, "h": pl.ANY}
    spec = lambda kind: pl.BlockSpec(memory_space=spaces[kind])
    many = isinstance(outs, tuple)
    out_kinds = out_kinds or "v" * (len(outs) if many else 1)
    out_specs = tuple(spec(k) for k in out_kinds)
    return pl.pallas_call(
        kernel,
        out_shape=outs,
        in_specs=[spec(k) for k in kinds],
        out_specs=out_specs if many else out_specs[0],
        scratch_shapes=list(scratch),
        compiler_params=pltpu.CompilerParams(vmem_limit_bytes=limit * 1024 * 1024),
    )(*args)


def shape(dims, dtype):
    return jax.ShapeDtypeStruct(dims, dtype)


def to_next(value, k):
    return lax.ppermute(value, "mp", [(i, (i + k) % N_MP) for i in range(N_MP)])


def to_other(value):
    size = lax.axis_size("dp")
    return lax.ppermute(value, "dp", [(i, i ^ 1) for i in range(size)])


def gathered(value):
    return [value] + [to_next(value, k) for k in range(1, N_MP)]


def after(value, *others):
    return lax.optimization_barrier((value, *others))[0]


def run_plan(plan, audio, w_input, e_rows):
    return call(
        plan_kernel,
        (
            shape((TABLE,), jnp.int32),
            shape((2 * ROWS, ROWS), bf16),
            shape((JOBS, MEL, WIN), bf16),
            shape((JOBS, MEL, BLOCK), bf16),
            shape((JOBS, 8, WIN), f32),
            shape((JOBS, ROWS, BLOCK), bf16),
            shape((JOBS, ROWS, WIN), bf16),
            shape((JOBS, WIN, ROWS), bf16),
            shape((JOBS, ROWS, BLOCK), bf16),
        ),
        "sss" + "v" * 7,
        (*plan, *audio, w_input, e_rows, plan[0].reshape(4, 128)),
        scratch=[VMEM((MEL, 640), bf16), VMEM((MEL, BLOCK), bf16)],
        out_kinds="s" + "v" * 8,
    )


def run_first(table, windows, wp):
    return call(
        first_kernel,
        (
            shape((D, ROWS), bf16),
            shape((D, ROWS), bf16),
            shape((ROWS, D), bf16),
            shape((JOBS, D + ROWS, BLOCK), bf16),
        ),
        "s" + "v" * 12,
        (table, *windows, *wp),
        scratch=work_shapes(),
        limit=MAIN_LIMIT,
    )


def work_shapes():
    return [VMEM((4, WIN, 256), bf16), VMEM((D, BLOCK), bf16), VMEM((D, WIN), bf16)]


def run_second(table, context, noise, valid, gram, first, wa_t, wm, wo):
    return call(
        second_kernel,
        (shape((JOBS, 2 * MEL, 128), bf16),) + (shape((JOBS, PIECE, 128), bf16),) * 4,
        "s" + "v" * 17,
        (table, context, noise, valid, gram, *first, wa_t, wm, *wo),
        scratch=work_shapes()
        + [
            VMEM((D + ROWS, BLOCK), bf16),
            VMEM((D + MEL, D + ROWS), bf16),
            VMEM((4 * PIECE, 128), bf16),
            VMEM((ROWS, BLOCK), bf16),
            VMEM((ROWS, WIN), bf16),
            VMEM((WIN, ROWS), bf16),
        ],
        limit=MAIN_LIMIT,
    )


def shards(
    mel_audio, start_noise, span_start, span_length, block_route,
    w_input, attn_gain, w_qkv, w_out, final_gain, w_mel,
):
    e_rows = jnp.asarray(time_rows())
    plan = (block_route, span_start, span_length)
    w3 = jnp.transpose(w_qkv, (1, 0, 2))
    whole, half = call(
        fold_kernel,
        (shape((3, ROWS, 256), bf16), shape((3, ROWS, 128), bf16)),
        "hhhh",
        (w_input, e_rows, attn_gain.reshape(1, D), w3),
        scratch=[
            VMEM((2 * MEL, D), bf16),
            VMEM((16, D), f32),
            VMEM((1, D), f32),
            VMEM((3, D, 256), bf16),
            pltpu.SemaphoreType.DMA((6,)),
        ],
        limit=60,
    )
    halves = gathered(half)[1:]
    mel_late, noise_late = after(mel_audio, half), after(start_noise, half)
    audio = (mel_audio, to_other(mel_late), start_noise, to_other(noise_late))
    table, gram, context, noise, valid, scaled, values, keys, own_win = run_plan(
        plan, audio, w_input, e_rows
    )
    wa_t, wo_t, wo_half, wm = call(
        prep_kernel,
        (
            shape((D, ROWS), bf16),
            shape((D, 256), bf16),
            shape((D, 128), bf16),
            shape((MEL, D), bf16),
        ),
        "vvvvv",
        (w_input, e_rows, after(w_out, table), w_mel, final_gain.reshape(1, D)),
    )
    out_halves = gathered(wo_half)[1:]
    *halves, _ = lax.optimization_barrier((*halves, wo_half))
    wp = [whole]
    for h in halves:
        wp += [h, to_other(h)]
    first = run_first(table, (valid, scaled, values, keys, own_win), wp)
    out_halves = lax.optimization_barrier((*out_halves, first[3]))
    first = (*first[:3], out_halves[-1])
    wo = [wo_t]
    for h in out_halves[:-1]:
        wo += [h, to_other(h)]
    tot, v0, v1, v2, v3 = run_second(table, context, noise, valid, gram, first, wa_t, wm, wo)
    pieces = [v0] + [to_next(v, k) for k, v in ((1, v1), (2, v2), (3, v3))]
    totals = gathered(after(tot, *pieces[1:]))
    pieces += [to_other(v) for v in pieces]
    packed = call(
        pack_kernel,
        shape((32, PIECE, 128), bf16),
        "s" + "h" * 8,
        (table, *pieces),
        scratch=[pltpu.SemaphoreType.DMA((8 * JOBS,))],
        out_kinds="h",
    )
    got = lax.all_to_all(packed, "dp", 0, 0, tiled=True)
    chosen = call(
        select_kernel,
        shape((WORK_DEV, PIECE, 128), bf16),
        "sh",
        (table, got),
        scratch=[pltpu.SemaphoreType.DMA((WORK_DEV,))],
        out_kinds="h",
    )
    parts = gathered(chosen)
    *totals, _ = lax.optimization_barrier((*totals, chosen))
    infilled = call(
        span_kernel,
        shape((UTT_DEV, MEL, SPAN_MAX), f32),
        "s" + "v" * 5,
        (table, *totals, to_other(jnp.concatenate(totals, axis=0))),
    )
    *parts, infilled = lax.optimization_barrier((*parts, infilled))
    velocity = call(
        final_kernel,
        shape((WORK_DEV, MEL, BLOCK), f32),
        "vvvv",
        tuple(parts),
        scratch=[VMEM((WORK_DEV, 4 * PIECE, 128), bf16)],
    )
    return (infilled, velocity)


def solution(mesh):
    return jax.shard_map(
        shards,
        mesh=mesh,
        in_specs=(
            P("dp", None, None),
            P("dp", None, None),
            P(),
            P(),
            P(),
            P(),
            P(),
            P(None, None, "mp"),
            P("mp", None),
            P(),
            P(),
        ),
        out_specs=(P("dp", None, None), P("dp", None, None)),
        check_vma=False,
    )
```

```python
import math

import jax
import jax.numpy as jnp
import numpy as np
from jax import lax
from jax.experimental import pallas as pl
from jax.experimental.pallas import tpu as pltpu
from jax.sharding import PartitionSpec as P

D = 1024
MEL = 80
HEAD_DIM = 64
HEADS = 16
BLOCK = 256
CTX = 128
BLK_UTT = 4
UTT_DEV = 4
WORK_DEV = 6
EULER = 2
FRAMES = 2048
WIN = 512
SPAN_MAX = 1024
SLOT_DEV = 16
N_MP = 4
JOBS = 4
ROWS = 176
PIECE = 48
flow_steps = 32.0
norm_eps = 1e-05
f32 = jnp.float32
bf16 = jnp.bfloat16
VMEM = pltpu.VMEM
SMEM = pltpu.SMEM
MAIN_LIMIT = 44
SLOT_AT, JOB_AT, COUNT_AT, OWNER_AT, TABLE = 32, 64, 68, 72, 80


def time_rows():
    half = D // 2
    freqs = np.exp(-math.log(10000.0) * np.arange(half, dtype=np.float32) / half)
    rows = np.zeros((16, D), np.float32)
    for step in range(EULER):
        angles = np.float32(1000.0 * step / flow_steps) * freqs.astype(np.float32)
        e = np.concatenate([np.sin(angles), np.cos(angles)])
        e = e - e.mean()
        rows[2 * step] = e
        rows[2 * step + 1] = e
    return rows


def high_low(rows):
    high = rows.astype(bf16).astype(f32)
    odd = lax.broadcasted_iota(jnp.int32, rows.shape, 0) % 2 == 1
    return jnp.where(odd, rows - high, high)


def fold_kernel(w_in_h, e_rows_h, gain_h, w_qkv_h, out, half, w_in, e_rows, gain, w_qkv, sems):
    pairs = [(w_in_h, w_in), (e_rows_h, e_rows), (gain_h, gain)]
    pairs += [(w_qkv_h.at[c], w_qkv.at[c]) for c in range(3)]
    copies = [pltpu.make_async_copy(a, b, sems.at[i]) for i, (a, b) in enumerate(pairs)]
    for copy in copies:
        copy.start()
    for copy in copies[0:3]:
        copy.wait()
    core = lax.axis_index("dp") & 1
    w = w_in[...].astype(f32)
    wc = w - jnp.mean(w, axis=1, keepdims=True)
    g = gain[...]
    wag = jnp.concatenate([wc * g, high_low(e_rows[...] * g)], axis=0).astype(bf16)
    for c in range(3):
        copies[3 + c].wait()
        res = jnp.dot(wag, w_qkv[c], preferred_element_type=f32)
        if c == 0:
            res = res * (math.log2(math.e) / math.sqrt(HEAD_DIM))
        e_res = res[160:176]
        row = lax.broadcasted_iota(jnp.int32, e_res.shape, 0)
        first = e_res[0:1] + e_res[1:2]
        second = e_res[2:3] + e_res[3:4]
        both = jnp.where(row < 2, first, jnp.where(row < 4, second, 0.0))
        out[c, 0:160, :] = res[0:160].astype(bf16)
        out[c, 160:176, :] = high_low(both).astype(bf16)
        half[c] = jnp.where(core == 0, out[c, :, 0:128], out[c, :, 128:256])


def prep_kernel(w_in, e_rows, w_out, w_mel, gain, wa_t, wo_t, half, wm):
    w = w_in[...].astype(f32)
    wc = w - jnp.mean(w, axis=1, keepdims=True)
    wa = jnp.concatenate([wc, high_low(e_rows[...]), jnp.zeros((80, D), f32)], axis=0)
    wa_t[...] = wa.T[:, :ROWS].astype(bf16)
    core = lax.axis_index("dp") & 1
    o = w_out[...].astype(f32)
    o = o - jnp.mean(o, axis=1, keepdims=True)
    wo_t[...] = o.T.astype(bf16)
    half[...] = jnp.where(core == 0, wo_t[:, 0:128], wo_t[:, 128:256])
    wm[...] = (w_mel[...].astype(f32) * gain[...]).astype(bf16)


def plan_kernel(
    route, starts, lengths, mel_a, mel_b, noise_a, noise_b, w_in, e_rows, route_v,
    table, gram, context_out, noise_out, valid_out, scaled_out, values_out, keys_out, own_out,
    chunk_s, x_s,
):
    dp = lax.axis_index("dp")
    m = lax.axis_index("mp")
    core = dp & 1
    w = w_in[...].astype(f32)
    wc = w - jnp.mean(w, axis=1, keepdims=True)
    wa = jnp.concatenate([wc, high_low(e_rows[...]), jnp.zeros((80, D), f32)], axis=0)
    wab = wa.astype(bf16)
    g = lax.dot_general(wab, wab, (((1,), (1,)), ((), ())), preferred_element_type=f32)
    g = g[0:ROWS, 0:ROWS] * (1.0 / D)
    high = g.astype(bf16)
    gram[0:ROWS, :] = high
    gram[ROWS : 2 * ROWS, :] = (g - high.astype(f32)).astype(bf16)
    base = (dp >> 1) * (2 * SLOT_DEV)
    seat = core * N_MP + m
    for i in range(TABLE):
        table[i] = -1

    def scan(s, rank):
        dest = route[base + s]
        live = dest >= 0
        q = rank >> 3

        @pl.when(jnp.logical_and(live, (rank & 7) == seat))
        def _():
            table[JOB_AT + q] = s

        @pl.when(jnp.logical_and(live, (s >> 4) == core))
        def _():
            away = ((rank >> 2) & 1) ^ core
            entry = (away * 4 + ((m - rank) & 3)) * JOBS + q
            table[entry] = (dest * 10923) >> 16
            table[SLOT_AT + entry] = s & 15

        return rank + live.astype(jnp.int32)

    n_live = lax.fori_loop(0, 2 * SLOT_DEV, scan, jnp.int32(0))
    n_jobs = (n_live - seat + 7) >> 3
    table[COUNT_AT] = n_jobs

    places = route_v[...]
    owner = (
        lax.broadcasted_iota(jnp.int32, places.shape, 0) * places.shape[1]
        + lax.broadcasted_iota(jnp.int32, places.shape, 1)
    ) >> 4
    for j in range(WORK_DEV):
        found = jnp.where(places == dp * WORK_DEV + j, owner, 0)
        table[OWNER_AT + j] = jnp.sum(found)

    def job(q, carry):
        s = table[JOB_AT + q]
        u = (s >> 2) & 3
        order = s & 3
        utter = (dp >> 1) * (2 * UTT_DEV) + (s >> 2)
        span = starts[utter]
        length = lengths[utter]
        first = span + BLOCK * order - CTX
        aligned = pl.multiple_of(jnp.clip((first >> 7) << 7, 0, FRAMES - 640), 128)
        off = pl.multiple_of(order * BLOCK, BLOCK)
        here = (s >> 4) == core

        @pl.when(here)
        def _():
            chunk_s[...] = mel_a[u, :, pl.ds(aligned, 640)]
            x_s[...] = noise_a[u, :, pl.ds(off, BLOCK)]

        @pl.when(jnp.logical_not(here))
        def _():
            chunk_s[...] = mel_b[u, :, pl.ds(aligned, 640)]
            x_s[...] = noise_b[u, :, pl.ds(off, BLOCK)]

        own = lax.broadcasted_iota(jnp.int32, (1, BLOCK), 1) < length - BLOCK * order
        x = jnp.where(own, x_s[...].astype(f32), 0.0)
        noise_out[q] = x.astype(bf16)
        shift = aligned - first
        shift = jnp.where(shift < 0, shift + 640, shift)
        chunk = pltpu.roll(chunk_s[...].astype(f32), shift, 1)[:, :WIN]
        pos = first + lax.broadcasted_iota(jnp.int32, (1, WIN), 1)
        valid = jnp.logical_and(pos >= 0, pos < FRAMES)
        in_span = jnp.logical_and(pos >= span, pos < span + length)
        keep = jnp.logical_and(valid, jnp.logical_not(in_span))
        context = jnp.where(keep, chunk, 0.0)
        context_out[q] = context.astype(bf16)
        valid = valid.astype(f32)
        in_block = jnp.logical_and(pos >= first + CTX, jnp.logical_and(pos < first + CTX + BLOCK, in_span))
        row = lax.broadcasted_iota(jnp.int32, (8, WIN), 0)
        valid_out[q] = jnp.where(row == 0, valid, in_block.astype(f32))
        window(0, context, valid, x, gram, scaled_out.at[q], values_out.at[q], keys_out.at[q], own_out.at[q])
        return carry

    lax.fori_loop(0, n_jobs, job, 0)


def window(n, context, valid, x, gram, scaled_out, values_out, keys_out, own_out):
    side = jnp.zeros((MEL, CTX), f32)
    state = jnp.concatenate([side, x.astype(bf16).astype(f32), side], axis=1)
    flags = (lax.broadcasted_iota(jnp.int32, (16, WIN), 0) >> 1) == n
    win = jnp.concatenate([context, state, flags.astype(f32)], axis=0)
    win = jnp.where(valid > 0.0, win, win[:, CTX : CTX + 1])
    win_b = win.astype(bf16)
    own_out[...] = win_b[:, CTX : CTX + BLOCK]
    gw = jnp.dot(gram[...], win_b, preferred_element_type=f32)
    var = jnp.sum(win * (gw[0:ROWS] + gw[ROWS : 2 * ROWS]), axis=0, keepdims=True)
    scaled = win * lax.rsqrt(jnp.maximum(var, 0.0) + norm_eps)
    scaled_out[...] = scaled[:, CTX : CTX + BLOCK].astype(bf16)
    values_out[...] = (scaled * valid).astype(bf16)
    padded = jnp.concatenate([scaled, jnp.zeros((256 - ROWS, WIN), f32)], axis=0)
    keys_out[...] = padded.T.astype(bf16)[:, :ROWS]


def attend(scaled, values, win_t, valid, weights, work, o_out):
    wq_s, wv_s, wk_s = weights
    k_s, q_s, v_s = work
    q_s[...] = jnp.dot(wq_s[...], scaled[...], preferred_element_type=f32).astype(bf16)
    keys = jnp.dot(win_t[...], wk_s[...], preferred_element_type=f32).astype(bf16)
    for p in range(4):
        k_s[p] = keys[:, 256 * p : 256 * p + 256]
    v_s[...] = jnp.dot(wv_s[...], values[...], preferred_element_type=f32).astype(bf16)
    ones_rows = jnp.broadcast_to(valid, (16, WIN)).astype(bf16)
    zero = jnp.zeros((HEAD_DIM, BLOCK), bf16)

    def score(g):
        columns = []
        for j in range(4):
            at = 256 * g + 64 * j
            rows = [q_s[at : at + 64, :] if t == j else zero for t in range(4)]
            columns.append(jnp.concatenate(rows, axis=0))
        return jnp.dot(k_s[g], jnp.concatenate(columns, axis=1), preferred_element_type=f32)

    ahead = score(0)
    for g in range(4):
        sc = ahead
        if g < 3:
            ahead = score(g + 1)
        top = jnp.max(sc, axis=0, keepdims=True)
        pr = jnp.exp2(sc - top).astype(bf16)
        for j in range(4):
            at = 256 * g + 64 * j
            lhs = jnp.concatenate([v_s[at : at + 64, :], ones_rows], axis=0)
            ov = jnp.dot(lhs, pr[:, 256 * j : 256 * j + 256], preferred_element_type=f32)
            o_out[at : at + 64, :] = (ov[0:64] / ov[64:65]).astype(bf16)


def velocity_of(wr_s, o, own):
    squares = jnp.zeros((8, BLOCK), f32)
    part = D // 4
    v = None
    for i in range(4):
        last = i == 3
        rows = slice(part * i, D + MEL if last else part * i + part)
        r = jnp.dot(wr_s[rows, :], o[...], preferred_element_type=f32)
        if last:
            v = r[part:]
            r = r[0:part]
        squares = squares + jnp.sum((r * r).reshape(part // 8, 8, BLOCK), axis=0)
    var = jnp.sum(squares, axis=0, keepdims=True) * (1.0 / D)
    return jnp.where(own, v * lax.rsqrt(var + norm_eps), 0.0)


def first_kernel(
    table, valid, scaled, values, keys, own_win,
    wp0, hp1, sp1, hp2, sp2, hp3, sp3,
    wq_s, wv_s, wk_s, o_out,
    k_s, q_s, v_s,
):
    at = 0
    for wp in (wp0, hp1, sp1, hp2, sp2, hp3, sp3):
        width = wp.shape[2]
        lanes = slice(at, at + width)
        pad = jnp.zeros((256 - ROWS, width), f32)
        wq_s[lanes, :] = jnp.concatenate([wp[0].astype(f32), pad], axis=0).T.astype(bf16)[:, :ROWS]
        wv_s[lanes, :] = jnp.concatenate([wp[2].astype(f32), pad], axis=0).T.astype(bf16)[:, :ROWS]
        wk_s[:, lanes] = wp[1]
        at += width

    def job(q, carry):
        o = o_out.at[q]
        o[1024 : 1024 + ROWS, :] = own_win[q]
        attend(
            scaled.at[q], values.at[q], keys.at[q], valid[q, 0:1, :],
            (wq_s, wv_s, wk_s), (k_s, q_s, v_s), o,
        )
        return carry

    lax.fori_loop(0, table[COUNT_AT], job, 0)


def second_kernel(
    table, context, noise, valid, gram, wq_s, wv_s, wk_s, o_in, wa_t, wm,
    wo0, ho1, so1, ho2, so2, ho3, so3,
    tot_out, v0, v1, v2, v3,
    k_s, q_s, v_s, o_s, wr_s, stage, scaled_s, values_s, keys_s,
):
    m = lax.axis_index("mp")
    at = 0
    for wo in (wo0, ho1, so1, ho2, so2, ho3, so3):
        width = wo.shape[1]
        wr_s[0:D, at : at + width] = wo[...]
        at += width
    wr_s[0:D, 1024 : 1024 + ROWS] = wa_t[...]
    wr_s[D : D + MEL, :] = jnp.dot(wm[...], wr_s[0:D, :], preferred_element_type=f32).astype(bf16)
    stage[...] = jnp.zeros(stage.shape, bf16)

    def job(q, carry):
        masks = valid[q]
        own = masks[1:2, CTX : CTX + BLOCK] > 0.0
        usable = masks[0:1, :]
        first = velocity_of(wr_s, o_in.at[q], own)
        x = noise[q].astype(f32) + first * (1.0 / flow_steps)
        window(
            1, context[q].astype(f32), usable, x, gram,
            scaled_s, values_s, keys_s, o_s.at[1024 : 1024 + ROWS, :],
        )
        attend(
            scaled_s, values_s, keys_s, usable, (wq_s, wv_s, wk_s), (k_s, q_s, v_s), o_s
        )
        last = velocity_of(wr_s, o_s, own)
        total = (first + last).astype(bf16)
        tot_out[q, 0:MEL, :] = total[:, 0:128]
        tot_out[q, MEL : 2 * MEL, :] = total[:, 128:256]
        vel = last.astype(bf16)
        stage[0:MEL, :] = vel[:, 0:128]
        stage[MEL : 2 * MEL, :] = vel[:, 128:256]
        for k, out in enumerate((v0, v1, v2, v3)):
            quarter = (m + k) & 3
            out[q] = stage[pl.ds(pl.multiple_of(quarter * PIECE, 16), PIECE), :]
        return carry

    lax.fori_loop(0, table[COUNT_AT], job, 0)


def pack_kernel(table, a0, a1, a2, a3, b0, b1, b2, b3, out, sems):
    def each(act):
        for i, a in enumerate((a0, a1, a2, a3, b0, b1, b2, b3)):
            for q in range(JOBS):
                entry = i * JOBS + q
                worker = table[entry]

                @pl.when(worker >= 0)
                def _():
                    act(pltpu.make_async_copy(a.at[q], out.at[worker], sems.at[entry]))

    each(lambda copy: copy.start())
    each(lambda copy: copy.wait())


def select_kernel(table, got, out, sems):
    copies = [
        pltpu.make_async_copy(got.at[table[OWNER_AT + j]], out.at[j], sems.at[j])
        for j in range(WORK_DEV)
    ]
    for copy in copies:
        copy.start()
    for copy in copies:
        copy.wait()


def span_kernel(table, a0, a1, a2, a3, b, out):
    out[...] = jnp.zeros(out.shape, f32)
    sources = [lambda q, a=a: a[q] for a in (a0, a1, a2, a3)]
    sources += [lambda q, k=k: b[k * JOBS + q] for k in range(N_MP)]
    for i, source in enumerate(sources):
        for q in range(JOBS):
            s = table[SLOT_AT + i * JOBS + q]

            @pl.when(s >= 0)
            def _():
                block = source(q).astype(f32)
                off = (s & 3) * BLOCK
                out[s >> 2, :, pl.ds(pl.multiple_of(off, 128), 128)] = block[0:MEL]
                out[s >> 2, :, pl.ds(pl.multiple_of(off + 128, 128), 128)] = block[MEL : 2 * MEL]


def final_kernel(b0, b1, b2, b3, out, stage):
    m = lax.axis_index("mp")
    for k, b in enumerate((b0, b1, b2, b3)):
        quarter = (m - k) & 3
        at = pl.multiple_of(quarter * PIECE, 16)
        for j in range(WORK_DEV):
            stage[j, pl.ds(at, PIECE), :] = b[j]
    for j in range(WORK_DEV):
        out[j, :, 0:128] = stage[j, 0:MEL, :].astype(f32)
        out[j, :, 128:256] = stage[j, MEL : 2 * MEL, :].astype(f32)


def call(kernel, outs, kinds, args, scratch=(), out_kinds=None, limit=24):
    spaces = {"s": SMEM, "v": VMEM, "h": pl.ANY}
    spec = lambda kind: pl.BlockSpec(memory_space=spaces[kind])
    many = isinstance(outs, tuple)
    out_kinds = out_kinds or "v" * (len(outs) if many else 1)
    out_specs = tuple(spec(k) for k in out_kinds)
    return pl.pallas_call(
        kernel,
        out_shape=outs,
        in_specs=[spec(k) for k in kinds],
        out_specs=out_specs if many else out_specs[0],
        scratch_shapes=list(scratch),
        compiler_params=pltpu.CompilerParams(vmem_limit_bytes=limit * 1024 * 1024),
    )(*args)


def shape(dims, dtype):
    return jax.ShapeDtypeStruct(dims, dtype)


def to_next(value, k):
    return lax.ppermute(value, "mp", [(i, (i + k) % N_MP) for i in range(N_MP)])


def to_other(value):
    size = lax.axis_size("dp")
    return lax.ppermute(value, "dp", [(i, i ^ 1) for i in range(size)])


def gathered(value):
    return [value] + [to_next(value, k) for k in range(1, N_MP)]


def after(value, *others):
    return lax.optimization_barrier((value, *others))[0]


def run_plan(plan, audio, w_input, e_rows):
    return call(
        plan_kernel,
        (
            shape((TABLE,), jnp.int32),
            shape((2 * ROWS, ROWS), bf16),
            shape((JOBS, MEL, WIN), bf16),
            shape((JOBS, MEL, BLOCK), bf16),
            shape((JOBS, 8, WIN), f32),
            shape((JOBS, ROWS, BLOCK), bf16),
            shape((JOBS, ROWS, WIN), bf16),
            shape((JOBS, WIN, ROWS), bf16),
            shape((JOBS, ROWS, BLOCK), bf16),
        ),
        "sss" + "v" * 7,
        (*plan, *audio, w_input, e_rows, plan[0].reshape(4, 128)),
        scratch=[VMEM((MEL, 640), bf16), VMEM((MEL, BLOCK), bf16)],
        out_kinds="s" + "v" * 8,
    )


def run_first(table, windows, wp):
    return call(
        first_kernel,
        (
            shape((D, ROWS), bf16),
            shape((D, ROWS), bf16),
            shape((ROWS, D), bf16),
            shape((JOBS, D + ROWS, BLOCK), bf16),
        ),
        "s" + "v" * 12,
        (table, *windows, *wp),
        scratch=work_shapes(),
        limit=MAIN_LIMIT,
    )


def work_shapes():
    return [VMEM((4, WIN, 256), bf16), VMEM((D, BLOCK), bf16), VMEM((D, WIN), bf16)]


def run_second(table, context, noise, valid, gram, first, wa_t, wm, wo):
    return call(
        second_kernel,
        (shape((JOBS, 2 * MEL, 128), bf16),) + (shape((JOBS, PIECE, 128), bf16),) * 4,
        "s" + "v" * 17,
        (table, context, noise, valid, gram, *first, wa_t, wm, *wo),
        scratch=work_shapes()
        + [
            VMEM((D + ROWS, BLOCK), bf16),
            VMEM((D + MEL, D + ROWS), bf16),
            VMEM((4 * PIECE, 128), bf16),
            VMEM((ROWS, BLOCK), bf16),
            VMEM((ROWS, WIN), bf16),
            VMEM((WIN, ROWS), bf16),
        ],
        limit=MAIN_LIMIT,
    )


def shards(
    mel_audio, start_noise, span_start, span_length, block_route,
    w_input, attn_gain, w_qkv, w_out, final_gain, w_mel,
):
    e_rows = jnp.asarray(time_rows())
    plan = (block_route, span_start, span_length)
    w3 = jnp.transpose(w_qkv, (1, 0, 2))
    whole, half = call(
        fold_kernel,
        (shape((3, ROWS, 256), bf16), shape((3, ROWS, 128), bf16)),
        "hhhh",
        (w_input, e_rows, attn_gain.reshape(1, D), w3),
        scratch=[
            VMEM((2 * MEL, D), bf16),
            VMEM((16, D), f32),
            VMEM((1, D), f32),
            VMEM((3, D, 256), bf16),
            pltpu.SemaphoreType.DMA((6,)),
        ],
        limit=60,
    )
    halves = gathered(half)[1:]
    mel_late, noise_late = after(mel_audio, half), after(start_noise, half)
    audio = (mel_late, to_other(mel_late), noise_late, to_other(noise_late))
    table, gram, context, noise, valid, scaled, values, keys, own_win = run_plan(
        plan, audio, w_input, e_rows
    )
    wa_t, wo_t, wo_half, wm = call(
        prep_kernel,
        (
            shape((D, ROWS), bf16),
            shape((D, 256), bf16),
            shape((D, 128), bf16),
            shape((MEL, D), bf16),
        ),
        "vvvvv",
        (w_input, e_rows, after(w_out, table), w_mel, final_gain.reshape(1, D)),
    )
    out_halves = gathered(wo_half)[1:]
    *halves, _ = lax.optimization_barrier((*halves, wo_half))
    wp = [whole]
    for h in halves:
        wp += [h, to_other(h)]
    first = run_first(table, (valid, scaled, values, keys, own_win), wp)
    out_halves = lax.optimization_barrier((*out_halves, first[3]))
    first = (*first[:3], out_halves[-1])
    wo = [wo_t]
    for h in out_halves[:-1]:
        wo += [h, to_other(h)]
    tot, v0, v1, v2, v3 = run_second(table, context, noise, valid, gram, first, wa_t, wm, wo)
    pieces = [v0] + [to_next(v, k) for k, v in ((1, v1), (2, v2), (3, v3))]
    totals = gathered(after(tot, *pieces[1:]))
    pieces += [to_other(v) for v in pieces]
    packed = call(
        pack_kernel,
        shape((32, PIECE, 128), bf16),
        "s" + "h" * 8,
        (table, *pieces),
        scratch=[pltpu.SemaphoreType.DMA((8 * JOBS,))],
        out_kinds="h",
    )
    got = lax.all_to_all(packed, "dp", 0, 0, tiled=True)
    chosen = call(
        select_kernel,
        shape((WORK_DEV, PIECE, 128), bf16),
        "sh",
        (table, got),
        scratch=[pltpu.SemaphoreType.DMA((WORK_DEV,))],
        out_kinds="h",
    )
    parts = gathered(chosen)
    *totals, _ = lax.optimization_barrier((*totals, chosen))
    infilled = call(
        span_kernel,
        shape((UTT_DEV, MEL, SPAN_MAX), f32),
        "s" + "v" * 5,
        (table, *totals, to_other(jnp.concatenate(totals, axis=0))),
    )
    *parts, infilled = lax.optimization_barrier((*parts, infilled))
    velocity = call(
        final_kernel,
        shape((WORK_DEV, MEL, BLOCK), f32),
        "vvvv",
        tuple(parts),
        scratch=[VMEM((WORK_DEV, 4 * PIECE, 128), bf16)],
    )
    return (infilled, velocity)


def solution(mesh):
    return jax.shard_map(
        shards,
        mesh=mesh,
        in_specs=(
            P("dp", None, None),
            P("dp", None, None),
            P(),
            P(),
            P(),
            P(),
            P(),
            P(None, None, "mp"),
            P("mp", None),
            P(),
            P(),
        ),
        out_specs=(P("dp", None, None), P("dp", None, None)),
        check_vma=False,
    )
```
